256 devices in a mesh: dp: 8 (over z), db: 32 (over y, x, core).
Axes of the slice: x: 4, y: 4, z: 8, core: 2. Of those that a mesh axis runs over, the one named last changes fastest.
Arguments:
- queries: bfloat16 [65536, 2048], P(('dp', 'db')), may hold values from -90 to 90
- grad_out: bfloat16 [65536, 2048], P(('dp', 'db')), may hold values from -6 to 6
- neighbour_ids: int32 [1024, 2], P(('dp', 'db')), may hold values from 0 to 255, as said below
- entry_home: int32 [256], replicated, may hold values from 0 to 255, as said below
- cache: bfloat16 [256, 128, 512], P('db'), may hold values from -6 to 6
- kv_weight: bfloat16 [512, 4096], replicated, may hold values from -0.25 to 0.25
Outputs:
- attended: bfloat16 [65536, 2048], P(('dp', 'db'))
- query_grad: bfloat16 [65536, 2048], P(('dp', 'db'))
- weight_grad: float32 [512, 4096], P(('dp', 'db'))
The draws below stay inside these ranges and needn't reach their ends.
Inputs may be any that keep to these rules, and one draw needn't show every extreme that they name: `neighbour_ids`: over the 4 stretches of one device at most 1 neighbours are stored on one shard (shard = entry_home[id] // 8), and some shard holds exactly 1 of them; the 2 neighbours of a stretch are stored on different shards. `entry_home`: A permutation: every position is taken once.
All inputs are finite; a program needn't handle non-finite values.
Results may differ from the reference program's by a relative error of at most 0.012.
The reference program's roundings to bfloat16 on the way (of `fetched`, `projected`, `probs_b`, `dscore` and `kv_grad`) count: a program that leaves them out, or rounds other values in their place, can miss the bound.
Values may be sent and summed in bfloat16 or wider, within the bound.
No kernel may reach another device: no remote copies, remote signals or barrier semaphores. Data moves between devices by JAX's collectives and lax.ppermute only.
A program may use at most 128 MiB of HBM per device.

```python
import jax
import jax.numpy as jnp
from jax import lax

HEADS = 16
DH = 128
DE = 512
NROWS = 128
STRETCH = 64
KNB = 2
CH_DEV = 4
ENT_DEV = 8
HD = 2048
STRETCHES = 1024
TOKENS = 65536
ENTRIES = 256
N_DB = 32


def home_table(key):
    return jax.random.permutation(jax.random.fold_in(key, 101), ENTRIES).astype(jnp.int32)


def draw_entry_home(key, part):
    return home_table(key)


def draw_neighbour_ids(key, part):
    home = home_table(key)
    key = jax.random.fold_in(key, 7)
    key_heat, key_pick, key_slot = jax.random.split(key, 3)
    blocks = STRETCHES // CH_DEV
    heat = jax.random.randint(key_heat, (N_DB,), 0, 1200)
    noise = jax.random.randint(key_pick, (blocks, N_DB), 0, 1000)
    score = (noise + heat[None, :]) * N_DB + jnp.arange(N_DB, dtype=jnp.int32)[None, :]
    chosen = jnp.argsort(-score, axis=1, stable=True)[:, :CH_DEV * KNB].astype(jnp.int32)
    shard = chosen.reshape(blocks, CH_DEV, KNB)
    local = jax.random.randint(key_slot, (blocks, CH_DEV, KNB), 0, ENT_DEV)
    spot = shard * ENT_DEV + local
    inverse = jnp.zeros((ENTRIES,), jnp.int32).at[home].set(jnp.arange(ENTRIES, dtype=jnp.int32))
    return inverse[spot].reshape(STRETCHES, KNB).astype(jnp.int32)


def draw_queries(key, part):
    key = jax.random.fold_in(key, 13)
    key_base = jax.random.fold_in(key, 0)
    values = jnp.clip(jax.random.normal(key_base, (TOKENS, HD), jnp.float32), -6.0, 6.0)
    return values.astype(jnp.bfloat16)


def block_scale(rng, dims, cuts, smallest, largest):
    gain = 1.0
    for dim, blocks in cuts:
        steps = jax.random.uniform(jax.random.fold_in(jax.random.fold_in(rng, 6), dim), (blocks,), jnp.float32, smallest / len(cuts), largest / len(cuts))
        gain = gain * jnp.repeat(jnp.exp(steps), dims[dim] // blocks).reshape((-1,) + (1,) * (len(dims) - 1 - dim))
    return gain


def normal_values(own_key, shape, spread, reach, cuts=(), held_as=jnp.bfloat16):
    array = jax.random.normal(own_key, shape, jnp.float32) * spread
    if len(cuts) > 0:
        array = block_scale(own_key, shape, cuts, -0.22, 0.18) * array
    return jnp.clip(array, min=-reach, max=reach).astype(held_as)


def setup_inputs(seed: int = 0) -> dict:
    streams_of = jax.random.split(jax.random.key(seed), 7)
    return {
        "queries": draw_queries(jax.random.fold_in(streams_of[6], 71), 0),
        "grad_out": normal_values(streams_of[1], (TOKENS, HD), 1.0, 6.0, ((0, 256),)),
        "neighbour_ids": draw_neighbour_ids(jax.random.fold_in(streams_of[6], 71), 0),
        "entry_home": draw_entry_home(jax.random.fold_in(streams_of[6], 71), 0),
        "cache": normal_values(streams_of[4], (ENTRIES, NROWS, DE), 1.0, 6.0, ((0, 32),)),
        "kv_weight": normal_values(streams_of[5], (DE, 2 * HD), DE ** -0.5, 0.25),
    }


def attention_pass(queries, grad_out, fetched, kv_weight):
    nchunk = queries.shape[0] // STRETCH
    keys_len = fetched.shape[0] // nchunk
    projected = jnp.dot(fetched, kv_weight, preferred_element_type=jnp.float32).astype(jnp.bfloat16)
    keys = projected[:, :HD].reshape(nchunk, keys_len, HEADS, DH).astype(jnp.float32)
    values = projected[:, HD:].reshape(nchunk, keys_len, HEADS, DH).astype(jnp.float32)
    query_h = queries.reshape(nchunk, STRETCH, HEADS, DH).astype(jnp.float32)
    grad_h = grad_out.reshape(nchunk, STRETCH, HEADS, DH).astype(jnp.float32)
    scale = DH ** -0.5
    scores = jnp.einsum("cqhd,ckhd->chqk", query_h, keys) * scale
    top = jnp.max(scores, axis=-1, keepdims=True)
    expo = jnp.exp(scores - top)
    probs = expo / jnp.sum(expo, axis=-1, keepdims=True)
    probs_b = probs.astype(jnp.bfloat16).astype(jnp.float32)
    context = jnp.einsum("chqk,ckhd->cqhd", probs_b, values)
    delta = jnp.sum(grad_h * context, axis=-1)
    dprob = jnp.einsum("cqhd,ckhd->chqk", grad_h, values)
    dscore = (probs * (dprob - jnp.transpose(delta, (0, 2, 1))[..., None])).astype(jnp.bfloat16).astype(jnp.float32)
    query_grad = (jnp.einsum("chqk,ckhd->cqhd", dscore, keys) * scale).astype(jnp.bfloat16)
    key_grad = jnp.einsum("chqk,cqhd->ckhd", dscore, query_h) * scale
    value_grad = jnp.einsum("chqk,cqhd->ckhd", probs_b, grad_h)
    kv_grad = jnp.concatenate([key_grad.reshape(-1, HD), value_grad.reshape(-1, HD)], axis=1).astype(jnp.bfloat16)
    attended = context.astype(jnp.bfloat16).reshape(-1, HD)
    return attended, query_grad.reshape(-1, HD), kv_grad


def reference(queries, grad_out, neighbour_ids, entry_home, cache, kv_weight):
    blocks = STRETCHES // CH_DEV
    span = CH_DEV * STRETCH
    q_blocks = queries.reshape(blocks, span, HD)
    g_blocks = grad_out.reshape(blocks, span, HD)
    id_blocks = neighbour_ids.reshape(blocks, CH_DEV * KNB)

    def step(total, inputs):
        q_blk, g_blk, id_blk = inputs
        position = entry_home[id_blk].astype(jnp.int32)
        fetched = cache[position].reshape(CH_DEV * KNB * NROWS, DE)
        attended, query_grad, kv_grad = attention_pass(q_blk, g_blk, fetched, kv_weight)
        term = lax.dot_general(fetched, kv_grad, (((0,), (0,)), ((), ())), preferred_element_type=jnp.float32)
        return total + term, (attended, query_grad)

    start = jnp.zeros((DE, 2 * HD), jnp.float32)
    total, (attended, query_grad) = lax.scan(step, start, (q_blocks, g_blocks, id_blocks))
    return attended.reshape(TOKENS, HD), query_grad.reshape(TOKENS, HD), total
```

```python
import functools

import jax
import jax.numpy as jnp
from jax import lax
from jax.experimental import pallas as pl
from jax.experimental.pallas import tpu as pltpu
from jax.sharding import Mesh, PartitionSpec as P

DH = 128
STRETCH = 64
NZ, NY, NX, NC = 8, 4, 4, 2
N_DB = NY * NX * NC
KEYS = 256
ROWS = 128
FEAT = 512
WANT = 8
PAIR = 2 * DH
STEPS = 32000.0
PARTS = 1
PAIRS = 2
WIDE = PAIRS * PAIR
RING = (0, 3, 1, 2)
TILE_R = 16
RB = ROWS // TILE_R
FB = FEAT // DH
NT = (((1,), (1,)), ((), ()))
TN = (((0,), (0,)), ((), ()))
ALL = ("z", "y", "x", "core")
PLANE = ("y", "x", "core")


def spread_kernel(coords_ref, ids_ref, home_ref, cache_ref, out_ref, sems):
    ents = cache_ref.shape[0]
    copies = []
    for rb in range(RB):
        for fb in range(FB):
            m = rb * FB + fb
            copies.append(
                pltpu.make_async_copy(
                    cache_ref.at[:, rb * TILE_R : (rb + 1) * TILE_R, fb * DH : (fb + 1) * DH],
                    out_ref.at[m, pl.ds(0, ents)],
                    sems.at[m],
                )
            )
    for cp in copies:
        cp.start()
    row = lax.broadcasted_iota(jnp.int32, (TILE_R, DH), 0)
    lane = lax.broadcasted_iota(jnp.int32, (TILE_R, DH), 1)
    tile = jnp.zeros((TILE_R, DH), jnp.float32)
    for k in range(WANT):
        spot = home_ref[ids_ref[k % 2, k // 2]].astype(jnp.float32)
        tile = jnp.where((row == 0) & (lane == k), spot, tile)
    tile = tile.astype(jnp.bfloat16)
    for m in range(RB * FB):
        out_ref[m, ents] = tile
    for cp in copies:
        cp.wait()


def pick_kernel(spots_ref, store_ref, out_ref):
    def one(d, carry):
        spots = [spots_ref[d, k] for k in range(WANT)]
        tiles = [store_ref[spot >> 3, spot & 7] for spot in spots]
        for k in range(WANT):
            out_ref[d * WANT + k] = tiles[k]
        return carry

    lax.fori_loop(0, out_ref.shape[0] // WANT, one, 0, unroll=8)


def encode(x):
    top = jnp.maximum(jnp.max(jnp.abs(x), axis=0, keepdims=True), 1e-36)
    power = jnp.ceil(jnp.log2(top))
    coded = jnp.round(x * jnp.exp2(-power) * STEPS).astype(jnp.int32)
    power = jnp.broadcast_to(power.astype(jnp.int32), (TILE_R, x.shape[1]))
    return coded.astype(jnp.int16), power.astype(jnp.int16)


def decode(ref):
    rows = ref.shape[0] - TILE_R
    power = ref[rows:, :].astype(jnp.int32)[:1].astype(jnp.float32)
    return ref[:rows, :].astype(jnp.int32).astype(jnp.float32) * (1.0 / STEPS) * jnp.exp2(power)


def put(ref, x):
    coded, power = encode(x)
    rows = ref.shape[0] - TILE_R
    ref[:rows, :] = coded
    ref[rows:, :] = power


def encode_rows(x):
    top = jnp.maximum(jnp.max(jnp.abs(x), axis=1, keepdims=True), 1e-36)
    power = jnp.ceil(jnp.log2(top))
    coded = jnp.round(x * jnp.exp2(-power) * STEPS).astype(jnp.int32)
    power = jnp.broadcast_to(power.astype(jnp.int32), (x.shape[0], DH))
    return coded.astype(jnp.int16), power.astype(jnp.int16)


def decode_rows(coded, power):
    power = power.astype(jnp.int32).astype(jnp.float32)[:, :1]
    return coded.astype(jnp.int32).astype(jnp.float32) * (1.0 / STEPS) * jnp.exp2(power)


def row_order(coords_ref):
    old = lax.broadcasted_iota(jnp.int32, (1, FEAT), 1)
    dx = ((old >> 2) & 3) ^ coords_ref[2]
    dy = ((old >> 4) & 3) ^ coords_ref[1]
    z = old >> 6
    px = jnp.where(dx == 3, 1, jnp.where(dx == 1, 2, jnp.where(dx == 2, 3, 0)))
    py = jnp.where(dy == 3, 1, jnp.where(dy == 1, 2, jnp.where(dy == 2, 3, 0)))
    core = coords_ref[3]
    first = jnp.where(core == 0, px, py)
    second = jnp.where(core == 0, py, px)
    place = first * 128 + second * 32 + z * 4 + (old & 3)
    new = lax.broadcasted_iota(jnp.int32, (FEAT, FEAT), 0)
    return jnp.where(new == place, 1.0, 0.0).astype(jnp.bfloat16)


def lay_rows(coords_ref, r_ref, rr_ref, f_ref, ft_ref, sems):
    copies = []
    for side, ref in enumerate((r_ref, rr_ref)):
        for rb in range(RB):
            for fb in range(FB):
                m = rb * FB + fb
                copies.append(
                    pltpu.make_async_copy(
                        ref.at[m],
                        f_ref.at[pl.ds(side * WANT, WANT), rb, :, fb * DH : (fb + 1) * DH],
                        sems.at[side * RB * FB + m],
                    )
                )
    copy_all(copies)
    f = f_ref[...].reshape(NC * WANT * ROWS, FEAT)
    ft_ref[...] = lax.dot_general(row_order(coords_ref), f, NT, preferred_element_type=jnp.float32).astype(
        jnp.bfloat16
    )


def first_kernel(coords_ref, r_ref, rr_ref, q_ref, g_ref, qg_ref, wk_ref, wv_ref, *refs):
    outs, f_ref, ft_ref, scratch, sems = refs[:6], refs[6], refs[7], refs[8:-1], refs[-1]

    @pl.when(pl.program_id(0) == 0)
    def _():
        lay_rows(coords_ref, r_ref, rr_ref, f_ref, ft_ref, sems)

    attend_kernel(coords_ref, f_ref, ft_ref, q_ref, g_ref, qg_ref, wk_ref, wv_ref, *outs, *scratch)


def attend_kernel(
    coords_ref, f_ref, ft_ref, q_ref, g_ref, qg_ref, wk_ref, wv_ref,
    own_ref, oth_ref, keepk_ref, sendk_ref, keepv_ref, sendv_ref,
    k_ref, v_ref, dk_ref, dv_ref,
):
    scale = DH ** (-0.5)
    tokens = q_ref.shape[0]
    every = NC * WANT * ROWS
    left = lax.broadcasted_iota(jnp.int32, (STRETCH, PAIR), 1) < DH
    zero = jnp.zeros((STRETCH, PAIR), jnp.bfloat16)
    f = f_ref[...].reshape(every, FEAT)

    def both(t):
        return jnp.concatenate([jnp.where(left, t, zero), jnp.where(left, zero, t)], axis=0)

    def query(s, cols):
        at = s * STRETCH
        ref, at = (q_ref, at) if at < tokens else (qg_ref, at - tokens)
        return both(ref[at : at + STRETCH, cols])

    def grad(s, cols):
        at = s * STRETCH
        ref = g_ref if at < tokens else qg_ref
        return both(ref[at : at + STRETCH, cols])

    def give(base, s, at_col, x):
        at = s * STRETCH
        ref, at = (own_ref, at) if at < tokens else (oth_ref, at - tokens)
        rows = slice(base + at, base + at + STRETCH)
        ref[rows, at_col : at_col + DH] = x[:STRETCH, :DH].astype(jnp.bfloat16)
        ref[rows, at_col + DH : at_col + PAIR] = x[STRETCH:, DH:].astype(jnp.bfloat16)

    items = [
        (s, slice(s * KEYS, (s + 1) * KEYS), slice(p * PAIR, (p + 1) * PAIR))
        for p in range(PAIRS)
        for s in range(NC * tokens // STRETCH)
    ]
    scores, dprob, pbs, ds = [], [], [], []
    k_ref[...] = jnp.dot(f, wk_ref[...], preferred_element_type=jnp.float32).astype(jnp.bfloat16)
    v_ref[...] = jnp.dot(f, wv_ref[...], preferred_element_type=jnp.float32).astype(jnp.bfloat16)
    for s, keys, cols in items:
        scores.append(
            lax.dot_general(k_ref[keys, cols], query(s, cols), NT, preferred_element_type=jnp.float32) * scale
        )
        dprob.append(lax.dot_general(v_ref[keys, cols], grad(s, cols), NT, preferred_element_type=jnp.float32))
    for x, dp in zip(scores, dprob):
        expo = jnp.exp(x - jnp.max(x, axis=0, keepdims=True))
        probs = expo * (1.0 / jnp.sum(expo, axis=0, keepdims=True))
        pb = probs.astype(jnp.bfloat16)
        delta = jnp.sum(pb.astype(jnp.float32) * dp, axis=0, keepdims=True)
        pbs.append(pb)
        ds.append((probs * (dp - delta)).astype(jnp.bfloat16))
    for i, (s, keys, cols) in enumerate(items):
        dv_ref[keys, cols] = jnp.dot(pbs[i], grad(s, cols), preferred_element_type=jnp.float32).astype(jnp.bfloat16)
        ctx = lax.dot_general(pbs[i], v_ref[keys, cols], TN, preferred_element_type=jnp.float32)
        give(0, s, cols.start, ctx)
    for i, (s, keys, cols) in enumerate(items):
        dk_ref[keys, cols] = (
            jnp.dot(ds[i], query(s, cols), preferred_element_type=jnp.float32) * scale
        ).astype(jnp.bfloat16)
        dq = lax.dot_general(ds[i], k_ref[keys, cols], TN, preferred_element_type=jnp.float32) * scale
        give(tokens, s, cols.start, dq)
    dwv = jnp.dot(ft_ref[...], dv_ref[...], preferred_element_type=jnp.float32)
    keepv_ref[:128, :] = dwv[:128]
    keepv_ref[128:, :] = dwv[256:384]
    put(sendv_ref, jnp.concatenate([dwv[128:256], dwv[384:]], axis=0))
    put(sendk_ref, jnp.dot(ft_ref[256:, :], dk_ref[...], preferred_element_type=jnp.float32))
    keepk_ref[...] = jnp.dot(ft_ref[:256, :], dk_ref[...], preferred_element_type=jnp.float32)


def attend(coords, rows, queries, grad_out, oth, kv_weight):
    tokens, width = queries.shape
    steps = width // WIDE // NC
    half = FEAT // 2
    every = NC * WANT * ROWS
    queries, grad_out, kv_weight = (
        pltpu.with_memory_space_constraint(a, pltpu.HBM) for a in (queries, grad_out, kv_weight)
    )
    mine = lambda rows, at0: pl.BlockSpec((rows, WIDE), lambda h, at: (0, at0 + at[3] * steps + h))
    col = lambda rows: pl.BlockSpec((rows, WIDE), lambda h, at: (0, h))
    shape = lambda rows, dtype: jax.ShapeDtypeStruct((rows, width // NC), dtype)
    return pl.pallas_call(
        first_kernel,
        grid_spec=pltpu.PrefetchScalarGridSpec(
            num_scalar_prefetch=1,
            grid=(steps,),
            in_specs=[pl.BlockSpec(memory_space=pl.ANY)] * 2
            + [mine(tokens, 0), mine(tokens, 0), col(2 * tokens), mine(FEAT, 0), mine(FEAT, NC * steps)],
            out_specs=[
                col(2 * tokens), col(2 * tokens),
                col(half), col(half + TILE_R), col(half), col(half + TILE_R),
            ],
            scratch_shapes=[
                pltpu.VMEM((NC * WANT, RB, TILE_R, FEAT), jnp.bfloat16),
                pltpu.VMEM((FEAT, every), jnp.bfloat16),
            ]
            + [pltpu.VMEM((every, WIDE), jnp.bfloat16)] * 4
            + [pltpu.SemaphoreType.DMA((NC * RB * FB,))],
        ),
        out_shape=[
            shape(2 * tokens, jnp.bfloat16), shape(2 * tokens, jnp.bfloat16),
            shape(half, jnp.float32), shape(half + TILE_R, jnp.int16),
            shape(half, jnp.float32), shape(half + TILE_R, jnp.int16),
        ],
        compiler_params=pltpu.CompilerParams(vmem_limit_bytes=36 * 2**20),
        cost_estimate=pl.CostEstimate(flops=11 * 10**9, bytes_accessed=8 * 2**20, transcendentals=10**6),
        name="attend",
    )(coords, *rows, queries, grad_out, oth, kv_weight, kv_weight)


def fold_kernel(kept_ref, came_ref, keep_ref, send_ref):
    rows = keep_ref.shape[0]
    total = kept_ref[...] + decode(came_ref)
    put(send_ref, total[rows:])
    keep_ref[...] = total[:rows]


def split_kernel(*refs):
    sums, keep_ref, send_refs = refs[: 4 * PARTS], refs[4 * PARTS], refs[4 * PARTS + 1 :]
    rows, width = keep_ref.shape
    wide = width // (2 * PARTS)
    for i in range(2 * PARTS):
        cols = slice(i * wide, (i + 1) * wide)
        total = sums[2 * i][...] + decode(sums[2 * i + 1])
        coded, power = encode_rows(total[rows:])
        for p, ref in enumerate(send_refs):
            ref[:, cols] = coded[p * rows : (p + 1) * rows]
            ref[:, width + i * DH : width + (i + 1) * DH] = power[p * rows : (p + 1) * rows]
        keep_ref[:, cols] = total[:rows]


def join_kernel(kept_ref, *refs):
    rows, width = kept_ref.shape
    wide = width // (2 * PARTS)
    parts = []
    for i in range(2 * PARTS):
        cols = slice(i * wide, (i + 1) * wide)
        total = kept_ref[:, cols]
        for ref in refs[:-1]:
            total = total + decode_rows(ref[:, cols], ref[:, width + i * DH : width + (i + 1) * DH])
        parts.append(total)
    total = jnp.concatenate(parts, axis=1)
    rows, wide = rows // NZ, width // 4
    for z in range(NZ):
        mine = total[z * rows : (z + 1) * rows]
        mine = jnp.concatenate([mine[:, q * wide : (q + 1) * wide] for q in range(4)], axis=0)
        refs[-1][z, :, :wide], refs[-1][z, :, wide:] = encode_rows(mine)


def z_kernel(got_ref, out_ref):
    wide = got_ref.shape[2] - DH
    total = None
    for z in range(NZ):
        piece = decode_rows(got_ref[z, :, :wide], got_ref[z, :, wide:])
        total = piece if z == 0 else total + piece
    rows = out_ref.shape[0]
    for q in range(4):
        out_ref[:, q * wide : (q + 1) * wide] = total[q * rows : (q + 1) * rows]


def copy_all(copies):
    for cp in copies:
        cp.start()
    for cp in copies:
        cp.wait()


def halves_kernel(coords_ref, q_ref, g_ref, out_ref, sems):
    tokens, width = q_ref.shape
    at = pl.multiple_of((1 - coords_ref[3]) * (width // NC), width // NC)
    copy_all(
        [
            pltpu.make_async_copy(ref.at[:, pl.ds(at, width // NC)], out_ref.at[pl.ds(i * tokens, tokens)], sems.at[i])
            for i, ref in enumerate((q_ref, g_ref))
        ]
    )


def place_kernel(coords_ref, *refs):
    srcs, (att_ref, dq_ref, sems) = refs[: 2 * PARTS], refs[2 * PARTS :]
    tokens, width = att_ref.shape
    wide = width // NC // PARTS
    copies = []
    for i, src in enumerate(srcs):
        core = coords_ref[3] if i < PARTS else 1 - coords_ref[3]
        at = pl.multiple_of(core * (width // NC) + i % PARTS * wide, wide)
        for j, dst in enumerate((att_ref, dq_ref)):
            copies.append(
                pltpu.make_async_copy(
                    src.at[pl.ds(j * tokens, tokens)], dst.at[:, pl.ds(at, wide)], sems.at[2 * i + j]
                )
            )
    copy_all(copies)


def local(kernel, name, out_shape, *args, coords=None, copies=0):
    space = pl.BlockSpec(memory_space=pl.ANY if copies else pltpu.VMEM)
    smem = [] if coords is None else [pl.BlockSpec(memory_space=pltpu.SMEM)]
    return pl.pallas_call(
        kernel,
        in_specs=smem + [space] * len(args),
        out_specs=jax.tree.map(lambda _: space, out_shape),
        out_shape=out_shape,
        scratch_shapes=[pltpu.SemaphoreType.DMA((copies,))] if copies else [],
        compiler_params=pltpu.CompilerParams(vmem_limit_bytes=16 * 2**20),
        name=name,
    )(*([] if coords is None else [coords]), *args)


def fetch(coords, neighbour_ids, entry_home, cache):
    ents = cache.shape[0]
    vmem = pl.BlockSpec(memory_space=pltpu.VMEM)
    smem = pl.BlockSpec(memory_space=pltpu.SMEM)
    pieces = pl.pallas_call(
        spread_kernel,
        in_specs=[smem, smem, smem, pl.BlockSpec(memory_space=pl.ANY)],
        out_specs=vmem,
        out_shape=jax.ShapeDtypeStruct((RB * FB, ents + 1, TILE_R, DH), jnp.bfloat16),
        scratch_shapes=[pltpu.SemaphoreType.DMA((RB * FB,))],
        compiler_params=pltpu.CompilerParams(vmem_limit_bytes=16 * 2**20),
        name="spread",
    )(
        coords,
        *(pltpu.with_memory_space_constraint(a, pltpu.HBM) for a in (neighbour_ids.T, entry_home, cache)),
    )
    store = lax.all_to_all(pieces, PLANE, split_axis=0, concat_axis=0, tiled=True)
    spots = store[:, ents, 0, :WANT].astype(jnp.int32)
    picked = pl.pallas_call(
        pick_kernel,
        in_specs=[smem, vmem],
        out_specs=vmem,
        out_shape=jax.ShapeDtypeStruct((N_DB * WANT, TILE_R, DH), jnp.bfloat16),
        compiler_params=pltpu.CompilerParams(vmem_limit_bytes=16 * 2**20),
        name="pick",
    )(spots, store)
    picked, coords = lax.optimization_barrier((picked, coords))
    answer = lax.all_to_all(
        picked.reshape(N_DB, WANT, TILE_R, DH), PLANE, split_axis=0, concat_axis=0, tiled=True
    )
    return answer, coords


def hops(mask, second):
    out = []
    for y in range(NY):
        for x in range(NX):
            for c in range(NC):
                to = (y, x ^ mask) if c == second else (y ^ mask, x)
                out.append(((y * NX + x) * NC + c, (to[0] * NX + to[1]) * NC + c))
    return out


def body(queries, grad_out, neighbour_ids, entry_home, cache, kv_weight):
    coords = jnp.stack([lax.axis_index(axis).astype(jnp.int32) for axis in ALL])
    tokens, width = queries.shape
    shape = jax.ShapeDtypeStruct
    swap = lambda v: lax.ppermute(v, "core", [(0, 1), (1, 0)])
    answer, coords = fetch(coords, neighbour_ids, entry_home, cache)
    hbm = lambda v: pltpu.with_memory_space_constraint(v, pltpu.HBM)
    theirs = shape((2 * tokens, width // NC), queries.dtype)
    oth = swap(local(halves_kernel, "halves", theirs, hbm(queries), hbm(grad_out), coords=coords, copies=2))
    half, quarter = FEAT // 2, FEAT // 4
    wide = width // NC // PARTS
    folded = [shape((quarter, wide), jnp.float32), shape((quarter + TILE_R, wide), jnp.int16)]
    tie = lax.optimization_barrier

    def one(keep_k, send_k, keep_v, send_v):
        return [keep_k, lax.ppermute(send_k, PLANE, hops(1, 0)), keep_v, lax.ppermute(send_v, PLANE, hops(3, 0))]

    def two(keep_k, came_k, keep_v, came_v):
        out = []
        for kept, came, mask in ((keep_k, came_k, 3), (keep_v, came_v, 1)):
            kept, sent = local(fold_kernel, "fold", folded, kept, came)
            out += [kept, lax.ppermute(sent, PLANE, hops(mask, 0))]
        return out

    args = (queries, grad_out, oth, kv_weight)
    own, other, *grads = attend(coords, (answer, swap(answer)), *args)
    sums = one(*grads)
    other = swap(other)
    sums = two(*sums)
    outs = [shape(queries.shape, queries.dtype)] * 2
    outs = local(place_kernel, "place", outs, own, other, coords=coords, copies=4)
    sums[3], outs = tie((sums[3], outs))
    part = quarter // 4
    shapes = [shape((part, width), jnp.float32)]
    shapes += [shape((part, width + 2 * PARTS * DH), jnp.int16)] * 3
    kept, *sent = local(split_kernel, "split", shapes, *sums)
    came = [lax.ppermute(v, PLANE, hops(mask, 1)) for v, mask in zip(sent, RING[1:])]
    pieces = local(join_kernel, "join", shape((NZ, 4 * part // NZ, width // 4 + DH), jnp.int16), kept, *came)
    got = lax.all_to_all(pieces, "z", split_axis=0, concat_axis=0, tiled=True)
    total = local(z_kernel, "zsum", shape((2 * NC, width), jnp.float32), got)
    core = lax.axis_index("core")
    mine = lax.dynamic_slice(total, (2 * core, 0), (2, width))
    came = swap(lax.dynamic_slice(total, (2 - 2 * core, 0), (2, width)))
    low, high = jnp.where(core == 0, mine, came), jnp.where(core == 0, came, mine)
    weight_grad = jnp.concatenate(
        [low[:, : width // 2], high[:, : width // 2], low[:, width // 2 :], high[:, width // 2 :]], axis=1
    )
    return (*outs, weight_grad)


def solution(mesh):
    grid = Mesh(mesh.devices.reshape(NZ, NY, NX, NC), ALL)
    return jax.shard_map(
        body,
        mesh=grid,
        in_specs=(P(ALL, None), P(ALL, None), P(ALL, None), P(), P(PLANE, None, None), P()),
        out_specs=(P(ALL, None), P(ALL, None), P(ALL, None)),
        check_vma=False,
    )
```

```python
import functools

import jax
import jax.numpy as jnp
from jax import lax
from jax.experimental import pallas as pl
from jax.experimental.pallas import tpu as pltpu
from jax.sharding import Mesh, PartitionSpec as P

DH = 128
STRETCH = 64
NZ, NY, NX, NC = 8, 4, 4, 2
N_DB = NY * NX * NC
KEYS = 256
ROWS = 128
FEAT = 512
WANT = 8
PAIR = 2 * DH
STEPS = 32000.0
PARTS = 1
PAIRS = 2
WIDE = PAIRS * PAIR
RING = (0, 3, 1, 2)
TILE_R = 16
RB = ROWS // TILE_R
FB = FEAT // DH
NT = (((1,), (1,)), ((), ()))
TN = (((0,), (0,)), ((), ()))
ALL = ("z", "y", "x", "core")
PLANE = ("y", "x", "core")


def spread_kernel(coords_ref, ids_hbm, home_hbm, cache_ref, out_ref, ids_ref, home_ref, sems):
    ents = cache_ref.shape[0]
    small = [
        pltpu.make_async_copy(ids_hbm, ids_ref, sems.at[RB * FB]),
        pltpu.make_async_copy(home_hbm, home_ref, sems.at[RB * FB + 1]),
    ]
    copies = []
    for rb in range(RB):
        for fb in range(FB):
            m = rb * FB + fb
            copies.append(
                pltpu.make_async_copy(
                    cache_ref.at[:, rb * TILE_R : (rb + 1) * TILE_R, fb * DH : (fb + 1) * DH],
                    out_ref.at[m, pl.ds(0, ents)],
                    sems.at[m],
                )
            )
    for cp in small + copies:
        cp.start()
    for cp in small:
        cp.wait()
    row = lax.broadcasted_iota(jnp.int32, (TILE_R, DH), 0)
    lane = lax.broadcasted_iota(jnp.int32, (TILE_R, DH), 1)
    tile = jnp.zeros((TILE_R, DH), jnp.float32)
    for k in range(WANT):
        spot = home_ref[ids_ref[k % 2, k // 2]].astype(jnp.float32)
        tile = jnp.where((row == 0) & (lane == k), spot, tile)
    tile = tile.astype(jnp.bfloat16)
    for m in range(RB * FB):
        out_ref[m, ents] = tile
    for cp in copies:
        cp.wait()


def pick_kernel(spots_ref, store_ref, out_ref):
    def one(d, carry):
        spots = [spots_ref[d, k] for k in range(WANT)]
        tiles = [store_ref[spot >> 3, spot & 7] for spot in spots]
        for k in range(WANT):
            out_ref[d * WANT + k] = tiles[k]
        return carry

    lax.fori_loop(0, out_ref.shape[0] // WANT, one, 0, unroll=8)


def encode(x):
    top = jnp.maximum(jnp.max(jnp.abs(x), axis=0, keepdims=True), 1e-36)
    power = jnp.ceil(jnp.log2(top))
    coded = jnp.round(x * jnp.exp2(-power) * STEPS).astype(jnp.int32)
    power = jnp.broadcast_to(power.astype(jnp.int32), (TILE_R, x.shape[1]))
    return coded.astype(jnp.int16), power.astype(jnp.int16)


def decode(ref):
    rows = ref.shape[0] - TILE_R
    power = ref[rows:, :].astype(jnp.int32)[:1].astype(jnp.float32)
    return ref[:rows, :].astype(jnp.int32).astype(jnp.float32) * (1.0 / STEPS) * jnp.exp2(power)


def put(ref, x):
    coded, power = encode(x)
    rows = ref.shape[0] - TILE_R
    ref[:rows, :] = coded
    ref[rows:, :] = power


def encode_rows(x):
    top = jnp.maximum(jnp.max(jnp.abs(x), axis=1, keepdims=True), 1e-36)
    power = jnp.ceil(jnp.log2(top))
    coded = jnp.round(x * jnp.exp2(-power) * STEPS).astype(jnp.int32)
    power = jnp.broadcast_to(power.astype(jnp.int32), (x.shape[0], DH))
    return coded.astype(jnp.int16), power.astype(jnp.int16)


def decode_rows(coded, power):
    power = power.astype(jnp.int32).astype(jnp.float32)[:, :1]
    return coded.astype(jnp.int32).astype(jnp.float32) * (1.0 / STEPS) * jnp.exp2(power)


def row_order(coords_ref):
    old = lax.broadcasted_iota(jnp.int32, (1, FEAT), 1)
    dx = ((old >> 2) & 3) ^ coords_ref[2]
    dy = ((old >> 4) & 3) ^ coords_ref[1]
    z = old >> 6
    px = jnp.where(dx == 3, 1, jnp.where(dx == 1, 2, jnp.where(dx == 2, 3, 0)))
    py = jnp.where(dy == 3, 1, jnp.where(dy == 1, 2, jnp.where(dy == 2, 3, 0)))
    core = coords_ref[3]
    first = jnp.where(core == 0, px, py)
    second = jnp.where(core == 0, py, px)
    place = first * 128 + second * 32 + z * 4 + (old & 3)
    new = lax.broadcasted_iota(jnp.int32, (FEAT, FEAT), 0)
    return jnp.where(new == place, 1.0, 0.0).astype(jnp.bfloat16)


def lay_rows(coords_ref, r_ref, rr_refs, f_ref, ft_ref):
    half = RB * FB // 2
    for side in range(NC):
        for rb in range(RB):
            for fb in range(FB):
                m = rb * FB + fb
                ref, at = (r_ref, m) if side == 0 else (rr_refs[m // half], m % half)
                for w in range(WANT):
                    f_ref[side * WANT + w, rb, :, fb * DH : (fb + 1) * DH] = ref[at, w]
    f = f_ref[...].reshape(NC * WANT * ROWS, FEAT)
    ft_ref[...] = lax.dot_general(row_order(coords_ref), f, NT, preferred_element_type=jnp.float32).astype(
        jnp.bfloat16
    )


def first_kernel(coords_ref, r_ref, rr0_ref, rr1_ref, q_ref, g_ref, qg_ref, wk_ref, wv_ref, *refs):
    outs, f_ref, ft_ref, scratch = refs[:6], refs[6], refs[7], refs[8:]

    @pl.when(pl.program_id(0) == 0)
    def _():
        lay_rows(coords_ref, r_ref, (rr0_ref, rr1_ref), f_ref, ft_ref)

    attend_kernel(coords_ref, f_ref, ft_ref, q_ref, g_ref, qg_ref, wk_ref, wv_ref, *outs, *scratch)


def attend_kernel(
    coords_ref, f_ref, ft_ref, q_ref, g_ref, qg_ref, wk_ref, wv_ref,
    own_ref, oth_ref, keepk_ref, sendk_ref, keepv_ref, sendv_ref,
    k_ref, v_ref, dk_ref, dv_ref,
):
    scale = DH ** (-0.5)
    tokens = q_ref.shape[0]
    every = NC * WANT * ROWS
    left = lax.broadcasted_iota(jnp.int32, (STRETCH, PAIR), 1) < DH
    zero = jnp.zeros((STRETCH, PAIR), jnp.bfloat16)
    f = f_ref[...].reshape(every, FEAT)

    def both(t):
        return jnp.concatenate([jnp.where(left, t, zero), jnp.where(left, zero, t)], axis=0)

    def query(s, cols):
        at = s * STRETCH
        ref, at = (q_ref, at) if at < tokens else (qg_ref, at - tokens)
        return both(ref[at : at + STRETCH, cols])

    def grad(s, cols):
        at = s * STRETCH
        ref = g_ref if at < tokens else qg_ref
        return both(ref[at : at + STRETCH, cols])

    def give(base, s, at_col, x):
        at = s * STRETCH
        ref, at = (own_ref, at) if at < tokens else (oth_ref, at - tokens)
        rows = slice(base + at, base + at + STRETCH)
        ref[rows, at_col : at_col + DH] = x[:STRETCH, :DH].astype(jnp.bfloat16)
        ref[rows, at_col + DH : at_col + PAIR] = x[STRETCH:, DH:].astype(jnp.bfloat16)

    items = [
        (s, slice(s * KEYS, (s + 1) * KEYS), slice(p * PAIR, (p + 1) * PAIR))
        for p in range(PAIRS)
        for s in range(NC * tokens // STRETCH)
    ]
    scores, dprob, pbs, ds = [], [], [], []
    k_ref[...] = jnp.dot(f, wk_ref[...], preferred_element_type=jnp.float32).astype(jnp.bfloat16)
    v_ref[...] = jnp.dot(f, wv_ref[...], preferred_element_type=jnp.float32).astype(jnp.bfloat16)
    for s, keys, cols in items:
        scores.append(
            lax.dot_general(k_ref[keys, cols], query(s, cols), NT, preferred_element_type=jnp.float32) * scale
        )
        dprob.append(lax.dot_general(v_ref[keys, cols], grad(s, cols), NT, preferred_element_type=jnp.float32))
    for x, dp in zip(scores, dprob):
        expo = jnp.exp(x - jnp.max(x, axis=0, keepdims=True))
        probs = expo * (1.0 / jnp.sum(expo, axis=0, keepdims=True))
        pb = probs.astype(jnp.bfloat16)
        delta = jnp.sum(pb.astype(jnp.float32) * dp, axis=0, keepdims=True)
        pbs.append(pb)
        ds.append((probs * (dp - delta)).astype(jnp.bfloat16))
    for i, (s, keys, cols) in enumerate(items):
        dv_ref[keys, cols] = jnp.dot(pbs[i], grad(s, cols), preferred_element_type=jnp.float32).astype(jnp.bfloat16)
        ctx = lax.dot_general(pbs[i], v_ref[keys, cols], TN, preferred_element_type=jnp.float32)
        give(0, s, cols.start, ctx)
    for i, (s, keys, cols) in enumerate(items):
        dk_ref[keys, cols] = (
            jnp.dot(ds[i], query(s, cols), preferred_element_type=jnp.float32) * scale
        ).astype(jnp.bfloat16)
        dq = lax.dot_general(ds[i], k_ref[keys, cols], TN, preferred_element_type=jnp.float32) * scale
        give(tokens, s, cols.start, dq)
    dwv = jnp.dot(ft_ref[...], dv_ref[...], preferred_element_type=jnp.float32)
    keepv_ref[:128, :] = dwv[:128]
    keepv_ref[128:, :] = dwv[256:384]
    put(sendv_ref, jnp.concatenate([dwv[128:256], dwv[384:]], axis=0))
    put(sendk_ref, jnp.dot(ft_ref[256:, :], dk_ref[...], preferred_element_type=jnp.float32))
    keepk_ref[...] = jnp.dot(ft_ref[:256, :], dk_ref[...], preferred_element_type=jnp.float32)


def attend(coords, rows, queries, grad_out, oth, kv_weight):
    tokens, width = queries.shape
    steps = width // WIDE // NC
    half = FEAT // 2
    every = NC * WANT * ROWS
    queries, grad_out, kv_weight = (
        pltpu.with_memory_space_constraint(a, pltpu.HBM) for a in (queries, grad_out, kv_weight)
    )
    mine = lambda rows, at0: pl.BlockSpec((rows, WIDE), lambda h, at: (0, at0 + at[3] * steps + h))
    col = lambda rows: pl.BlockSpec((rows, WIDE), lambda h, at: (0, h))
    shape = lambda rows, dtype: jax.ShapeDtypeStruct((rows, width // NC), dtype)
    return pl.pallas_call(
        first_kernel,
        grid_spec=pltpu.PrefetchScalarGridSpec(
            num_scalar_prefetch=1,
            grid=(steps,),
            in_specs=[pl.BlockSpec(memory_space=pltpu.VMEM)] * 3
            + [mine(tokens, 0), mine(tokens, 0), col(2 * tokens), mine(FEAT, 0), mine(FEAT, NC * steps)],
            out_specs=[
                col(2 * tokens), col(2 * tokens),
                col(half), col(half + TILE_R), col(half), col(half + TILE_R),
            ],
            scratch_shapes=[
                pltpu.VMEM((NC * WANT, RB, TILE_R, FEAT), jnp.bfloat16),
                pltpu.VMEM((FEAT, every), jnp.bfloat16),
            ]
            + [pltpu.VMEM((every, WIDE), jnp.bfloat16)] * 4,
        ),
        out_shape=[
            shape(2 * tokens, jnp.bfloat16), shape(2 * tokens, jnp.bfloat16),
            shape(half, jnp.float32), shape(half + TILE_R, jnp.int16),
            shape(half, jnp.float32), shape(half + TILE_R, jnp.int16),
        ],
        compiler_params=pltpu.CompilerParams(vmem_limit_bytes=36 * 2**20),
        cost_estimate=pl.CostEstimate(flops=11 * 10**9, bytes_accessed=8 * 2**20, transcendentals=10**6),
        name="attend",
    )(coords, *rows, queries, grad_out, oth, kv_weight, kv_weight)


def fold_kernel(kept_ref, came_ref, keep_ref, send_ref):
    rows = keep_ref.shape[0]
    total = kept_ref[...] + decode(came_ref)
    put(send_ref, total[rows:])
    keep_ref[...] = total[:rows]


def split_kernel(*refs):
    sums, keep_ref, send_refs = refs[: 4 * PARTS], refs[4 * PARTS], refs[4 * PARTS + 1 :]
    rows, width = keep_ref.shape
    wide = width // (2 * PARTS)
    for i in range(2 * PARTS):
        cols = slice(i * wide, (i + 1) * wide)
        total = sums[2 * i][...] + decode(sums[2 * i + 1])
        coded, power = encode_rows(total[rows:])
        for p, ref in enumerate(send_refs):
            ref[:, cols] = coded[p * rows : (p + 1) * rows]
            ref[:, width + i * DH : width + (i + 1) * DH] = power[p * rows : (p + 1) * rows]
        keep_ref[:, cols] = total[:rows]


def join_kernel(kept_ref, *refs):
    rows, width = kept_ref.shape
    wide = width // (2 * PARTS)
    parts = []
    for i in range(2 * PARTS):
        cols = slice(i * wide, (i + 1) * wide)
        total = kept_ref[:, cols]
        for ref in refs[:-1]:
            total = total + decode_rows(ref[:, cols], ref[:, width + i * DH : width + (i + 1) * DH])
        parts.append(total)
    total = jnp.concatenate(parts, axis=1)
    rows, wide = rows // NZ, width // 4
    for z in range(NZ):
        mine = total[z * rows : (z + 1) * rows]
        mine = jnp.concatenate([mine[:, q * wide : (q + 1) * wide] for q in range(4)], axis=0)
        refs[-1][z, :, :wide], refs[-1][z, :, wide:] = encode_rows(mine)


def z_kernel(got_ref, out_ref):
    wide = got_ref.shape[2] - DH
    total = None
    for z in range(NZ):
        piece = decode_rows(got_ref[z, :, :wide], got_ref[z, :, wide:])
        total = piece if z == 0 else total + piece
    rows = out_ref.shape[0]
    for q in range(4):
        out_ref[:, q * wide : (q + 1) * wide] = total[q * rows : (q + 1) * rows]


def copy_all(copies):
    for cp in copies:
        cp.start()
    for cp in copies:
        cp.wait()


def halves_kernel(coords_ref, q_ref, g_ref, out_ref, sems):
    tokens, width = q_ref.shape
    at = pl.multiple_of((1 - coords_ref[3]) * (width // NC), width // NC)
    copy_all(
        [
            pltpu.make_async_copy(ref.at[:, pl.ds(at, width // NC)], out_ref.at[pl.ds(i * tokens, tokens)], sems.at[i])
            for i, ref in enumerate((q_ref, g_ref))
        ]
    )


def place_kernel(coords_ref, *refs):
    srcs, (att_ref, dq_ref, sems) = refs[: 2 * PARTS], refs[2 * PARTS :]
    tokens, width = att_ref.shape
    wide = width // NC // PARTS
    copies = []
    for i, src in enumerate(srcs):
        core = coords_ref[3] if i < PARTS else 1 - coords_ref[3]
        at = pl.multiple_of(core * (width // NC) + i % PARTS * wide, wide)
        for j, dst in enumerate((att_ref, dq_ref)):
            copies.append(
                pltpu.make_async_copy(
                    src.at[pl.ds(j * tokens, tokens)], dst.at[:, pl.ds(at, wide)], sems.at[2 * i + j]
                )
            )
    copy_all(copies)


def local(kernel, name, out_shape, *args, coords=None, copies=0):
    space = pl.BlockSpec(memory_space=pl.ANY if copies else pltpu.VMEM)
    smem = [] if coords is None else [pl.BlockSpec(memory_space=pltpu.SMEM)]
    return pl.pallas_call(
        kernel,
        in_specs=smem + [space] * len(args),
        out_specs=jax.tree.map(lambda _: space, out_shape),
        out_shape=out_shape,
        scratch_shapes=[pltpu.SemaphoreType.DMA((copies,))] if copies else [],
        compiler_params=pltpu.CompilerParams(vmem_limit_bytes=16 * 2**20),
        name=name,
    )(*([] if coords is None else [coords]), *args)


def fetch(coords, neighbour_ids, entry_home, cache):
    ents = cache.shape[0]
    vmem = pl.BlockSpec(memory_space=pltpu.VMEM)
    smem = pl.BlockSpec(memory_space=pltpu.SMEM)
    pieces = pl.pallas_call(
        spread_kernel,
        in_specs=[pl.BlockSpec(memory_space=pl.ANY)] * 4,
        out_specs=vmem,
        out_shape=jax.ShapeDtypeStruct((RB * FB, ents + 1, TILE_R, DH), jnp.bfloat16),
        scratch_shapes=[
            pltpu.SMEM(neighbour_ids.shape[::-1], jnp.int32),
            pltpu.SMEM(entry_home.shape, jnp.int32),
            pltpu.SemaphoreType.DMA((RB * FB + 2,)),
        ],
        compiler_params=pltpu.CompilerParams(vmem_limit_bytes=16 * 2**20),
        name="spread",
    )(
        coords,
        *(pltpu.with_memory_space_constraint(a, pltpu.HBM) for a in (neighbour_ids.T, entry_home, cache)),
    )
    store = lax.all_to_all(pieces, PLANE, split_axis=0, concat_axis=0, tiled=True)
    spots = store[:, ents, 0, :WANT].astype(jnp.int32)
    picked = pl.pallas_call(
        pick_kernel,
        in_specs=[smem, vmem],
        out_specs=vmem,
        out_shape=pltpu.VMEM((N_DB * WANT, TILE_R, DH), jnp.bfloat16),
        compiler_params=pltpu.CompilerParams(vmem_limit_bytes=16 * 2**20),
        name="pick",
    )(spots, store)
    picked, coords = lax.optimization_barrier((picked, coords))
    answer = lax.all_to_all(
        picked.reshape(N_DB, WANT, TILE_R, DH), PLANE, split_axis=0, concat_axis=0, tiled=True
    )
    return answer, coords


def hops(mask, second):
    out = []
    for y in range(NY):
        for x in range(NX):
            for c in range(NC):
                to = (y, x ^ mask) if c == second else (y ^ mask, x)
                out.append(((y * NX + x) * NC + c, (to[0] * NX + to[1]) * NC + c))
    return out


def body(queries, grad_out, neighbour_ids, entry_home, cache, kv_weight):
    coords = jnp.stack([lax.axis_index(axis).astype(jnp.int32) for axis in ALL])
    tokens, width = queries.shape
    shape = jax.ShapeDtypeStruct
    swap = lambda v: lax.ppermute(v, "core", [(0, 1), (1, 0)])
    answer, coords = fetch(coords, neighbour_ids, entry_home, cache)
    hbm = lambda v: pltpu.with_memory_space_constraint(v, pltpu.HBM)
    theirs = shape((2 * tokens, width // NC), queries.dtype)
    oth = swap(local(halves_kernel, "halves", theirs, hbm(queries), hbm(grad_out), coords=coords, copies=2))
    half, quarter = FEAT // 2, FEAT // 4
    wide = width // NC // PARTS
    folded = [shape((quarter, wide), jnp.float32), shape((quarter + TILE_R, wide), jnp.int16)]
    tie = lax.optimization_barrier

    def one(keep_k, send_k, keep_v, send_v):
        return [keep_k, lax.ppermute(send_k, PLANE, hops(1, 0)), keep_v, lax.ppermute(send_v, PLANE, hops(3, 0))]

    def two(keep_k, came_k, keep_v, came_v):
        out = []
        for kept, came, mask in ((keep_k, came_k, 3), (keep_v, came_v, 1)):
            kept, sent = local(fold_kernel, "fold", folded, kept, came)
            out += [kept, lax.ppermute(sent, PLANE, hops(mask, 0))]
        return out

    args = (queries, grad_out, oth, kv_weight)
    own, other, *grads = attend(coords, (answer, swap(answer[:16]), swap(answer[16:])), *args)
    sums = one(*grads)
    other = swap(other)
    sums = two(*sums)
    outs = [shape(queries.shape, queries.dtype)] * 2
    outs = local(place_kernel, "place", outs, own, other, coords=coords, copies=4)
    sums[3], outs = tie((sums[3], outs))
    part = quarter // 4
    shapes = [shape((part, width), jnp.float32)]
    shapes += [shape((part, width + 2 * PARTS * DH), jnp.int16)] * 3
    kept, *sent = local(split_kernel, "split", shapes, *sums)
    came = [lax.ppermute(v, PLANE, hops(mask, 1)) for v, mask in zip(sent, RING[1:])]
    pieces = local(join_kernel, "join", shape((NZ, 4 * part // NZ, width // 4 + DH), jnp.int16), kept, *came)
    got = lax.all_to_all(pieces, "z", split_axis=0, concat_axis=0, tiled=True)
    total = local(z_kernel, "zsum", shape((2 * NC, width), jnp.float32), got)
    core = lax.axis_index("core")
    mine = lax.dynamic_slice(total, (2 * core, 0), (2, width))
    came = swap(lax.dynamic_slice(total, (2 - 2 * core, 0), (2, width)))
    low, high = jnp.where(core == 0, mine, came), jnp.where(core == 0, came, mine)
    weight_grad = jnp.concatenate(
        [low[:, : width // 2], high[:, : width // 2], low[:, width // 2 :], high[:, width // 2 :]], axis=1
    )
    return (*outs, weight_grad)


def solution(mesh):
    grid = Mesh(mesh.devices.reshape(NZ, NY, NX, NC), ALL)
    return jax.shard_map(
        body,
        mesh=grid,
        in_specs=(P(ALL, None), P(ALL, None), P(ALL, None), P(), P(PLANE, None, None), P()),
        out_specs=(P(ALL, None), P(ALL, None), P(ALL, None)),
        check_vma=False,
    )
```

```python
import functools

import jax
import jax.numpy as jnp
from jax import lax
from jax.experimental import pallas as pl
from jax.experimental.pallas import tpu as pltpu
from jax.sharding import Mesh, PartitionSpec as P

DH = 128
STRETCH = 64
NZ, NY, NX, NC = 8, 4, 4, 2
N_DB = NY * NX * NC
KEYS = 256
ROWS = 128
FEAT = 512
WANT = 8
PAIR = 2 * DH
STEPS = 32000.0
PARTS = 1
PAIRS = 2
WIDE = PAIRS * PAIR
RING = (0, 3, 1, 2)
TILE_R = 16
RB = ROWS // TILE_R
FB = FEAT // DH
NT = (((1,), (1,)), ((), ()))
TN = (((0,), (0,)), ((), ()))
ALL = ("z", "y", "x", "core")
PLANE = ("y", "x", "core")


def spread_kernel(coords_ref, ids_hbm, home_hbm, cache_ref, out_ref, ids_ref, home_ref, sems):
    ents = cache_ref.shape[0]
    small = [
        pltpu.make_async_copy(ids_hbm, ids_ref, sems.at[RB * FB]),
        pltpu.make_async_copy(home_hbm, home_ref, sems.at[RB * FB + 1]),
    ]
    copies = []
    for rb in range(RB):
        for fb in range(FB):
            m = rb * FB + fb
            copies.append(
                pltpu.make_async_copy(
                    cache_ref.at[:, rb * TILE_R : (rb + 1) * TILE_R, fb * DH : (fb + 1) * DH],
                    out_ref.at[m, pl.ds(0, ents)],
                    sems.at[m],
                )
            )
    for cp in small + copies:
        cp.start()
    for cp in small:
        cp.wait()
    row = lax.broadcasted_iota(jnp.int32, (TILE_R, DH), 0)
    lane = lax.broadcasted_iota(jnp.int32, (TILE_R, DH), 1)
    tile = jnp.zeros((TILE_R, DH), jnp.float32)
    for k in range(WANT):
        spot = home_ref[ids_ref[k % 2, k // 2]].astype(jnp.float32)
        tile = jnp.where((row == 0) & (lane == k), spot, tile)
    tile = tile.astype(jnp.bfloat16)
    for m in range(RB * FB):
        out_ref[m, ents] = tile
    for cp in copies:
        cp.wait()


def pick_kernel(spots_ref, store_ref, out_ref):
    batch = 4

    def some(d, carry):
        spots = [spots_ref[d * batch + i, k] for i in range(batch) for k in range(WANT)]
        tiles = [store_ref[spot >> 3, spot & 7] for spot in spots]
        for i, tile in enumerate(tiles):
            out_ref[d * batch * WANT + i] = tile
        return carry

    lax.fori_loop(0, N_DB // batch, some, 0, unroll=2)


def encode(x):
    top = jnp.maximum(jnp.max(jnp.abs(x), axis=0, keepdims=True), 1e-36)
    power = jnp.ceil(jnp.log2(top))
    coded = jnp.round(x * jnp.exp2(-power) * STEPS).astype(jnp.int32)
    power = jnp.broadcast_to(power.astype(jnp.int32), (TILE_R, x.shape[1]))
    return coded.astype(jnp.int16), power.astype(jnp.int16)


def decode(ref):
    rows = ref.shape[0] - TILE_R
    power = ref[rows:, :].astype(jnp.int32)[:1].astype(jnp.float32)
    return ref[:rows, :].astype(jnp.int32).astype(jnp.float32) * (1.0 / STEPS) * jnp.exp2(power)


def put(ref, x):
    coded, power = encode(x)
    rows = ref.shape[0] - TILE_R
    ref[:rows, :] = coded
    ref[rows:, :] = power


def encode_rows(x):
    top = jnp.maximum(jnp.max(jnp.abs(x), axis=1, keepdims=True), 1e-36)
    power = jnp.ceil(jnp.log2(top))
    coded = jnp.round(x * jnp.exp2(-power) * STEPS).astype(jnp.int32)
    power = jnp.broadcast_to(power.astype(jnp.int32), (x.shape[0], DH))
    return coded.astype(jnp.int16), power.astype(jnp.int16)


def decode_rows(coded, power):
    power = power.astype(jnp.int32).astype(jnp.float32)[:, :1]
    return coded.astype(jnp.int32).astype(jnp.float32) * (1.0 / STEPS) * jnp.exp2(power)


def row_order(coords_ref):
    old = lax.broadcasted_iota(jnp.int32, (1, FEAT), 1)
    dx = ((old >> 2) & 3) ^ coords_ref[2]
    dy = ((old >> 4) & 3) ^ coords_ref[1]
    z = old >> 6
    px = jnp.where(dx == 3, 1, jnp.where(dx == 1, 2, jnp.where(dx == 2, 3, 0)))
    py = jnp.where(dy == 3, 1, jnp.where(dy == 1, 2, jnp.where(dy == 2, 3, 0)))
    core = coords_ref[3]
    first = jnp.where(core == 0, px, py)
    second = jnp.where(core == 0, py, px)
    place = first * 128 + second * 32 + z * 4 + (old & 3)
    new = lax.broadcasted_iota(jnp.int32, (FEAT, FEAT), 0)
    return jnp.where(new == place, 1.0, 0.0).astype(jnp.bfloat16)


def lay_rows(coords_ref, r_ref, rr_refs, f_ref, ft_ref):
    half = RB * FB // 2
    for side in range(NC):
        for rb in range(RB):
            for fb in range(FB):
                m = rb * FB + fb
                ref, at = (r_ref, m) if side == 0 else (rr_refs[m // half], m % half)
                for w in range(WANT):
                    f_ref[side * WANT + w, rb, :, fb * DH : (fb + 1) * DH] = ref[at, w]
    f = f_ref[...].reshape(NC * WANT * ROWS, FEAT)
    ft_ref[...] = lax.dot_general(row_order(coords_ref), f, NT, preferred_element_type=jnp.float32).astype(
        jnp.bfloat16
    )


def first_kernel(coords_ref, r_ref, rr0_ref, rr1_ref, q_ref, g_ref, qg_ref, wk_ref, wv_ref, *refs):
    outs, f_ref, ft_ref, scratch = refs[:6], refs[6], refs[7], refs[8:]

    @pl.when(pl.program_id(0) == 0)
    def _():
        lay_rows(coords_ref, r_ref, (rr0_ref, rr1_ref), f_ref, ft_ref)

    attend_kernel(coords_ref, f_ref, ft_ref, q_ref, g_ref, qg_ref, wk_ref, wv_ref, *outs, *scratch)


def attend_kernel(
    coords_ref, f_ref, ft_ref, q_ref, g_ref, qg_ref, wk_ref, wv_ref,
    own_ref, oth_ref, keepk_ref, sendk_ref, keepv_ref, sendv_ref,
    k_ref, v_ref, dk_ref, dv_ref,
):
    scale = DH ** (-0.5)
    tokens = q_ref.shape[0]
    every = NC * WANT * ROWS
    left = lax.broadcasted_iota(jnp.int32, (STRETCH, PAIR), 1) < DH
    zero = jnp.zeros((STRETCH, PAIR), jnp.bfloat16)
    f = f_ref[...].reshape(every, FEAT)

    def both(t):
        return jnp.concatenate([jnp.where(left, t, zero), jnp.where(left, zero, t)], axis=0)

    def query(s, cols):
        at = s * STRETCH
        ref, at = (q_ref, at) if at < tokens else (qg_ref, at - tokens)
        return both(ref[at : at + STRETCH, cols])

    def grad(s, cols):
        at = s * STRETCH
        ref = g_ref if at < tokens else qg_ref
        return both(ref[at : at + STRETCH, cols])

    def give(base, s, at_col, x):
        at = s * STRETCH
        ref, at = (own_ref, at) if at < tokens else (oth_ref, at - tokens)
        rows = slice(base + at, base + at + STRETCH)
        ref[rows, at_col : at_col + DH] = x[:STRETCH, :DH].astype(jnp.bfloat16)
        ref[rows, at_col + DH : at_col + PAIR] = x[STRETCH:, DH:].astype(jnp.bfloat16)

    items = [
        (s, slice(s * KEYS, (s + 1) * KEYS), slice(p * PAIR, (p + 1) * PAIR))
        for p in range(PAIRS)
        for s in range(NC * tokens // STRETCH)
    ]
    k_ref[...] = jnp.dot(f, wk_ref[...], preferred_element_type=jnp.float32).astype(jnp.bfloat16)
    v_ref[...] = jnp.dot(f, wv_ref[...], preferred_element_type=jnp.float32).astype(jnp.bfloat16)

    def score(item):
        s, keys, cols = item
        scores = lax.dot_general(query(s, cols), k_ref[keys, cols], NT, preferred_element_type=jnp.float32) * scale
        return scores, lax.dot_general(grad(s, cols), v_ref[keys, cols], NT, preferred_element_type=jnp.float32)

    def soften(x, dp):
        expo = jnp.exp(x - jnp.max(x, axis=1, keepdims=True))
        probs = expo * (1.0 / jnp.sum(expo, axis=1, keepdims=True))
        pb = probs.astype(jnp.bfloat16)
        delta = jnp.sum(pb.astype(jnp.float32) * dp, axis=1, keepdims=True)
        return pb, (probs * (dp - delta)).astype(jnp.bfloat16)

    def value_side(item, pb):
        s, keys, cols = item
        give(0, s, cols.start, jnp.dot(pb, v_ref[keys, cols], preferred_element_type=jnp.float32))
        dv = lax.dot_general(pb, grad(s, cols), TN, preferred_element_type=jnp.float32)
        dv_ref[keys, cols] = dv.astype(jnp.bfloat16)

    def key_side(item, ds):
        s, keys, cols = item
        dk = lax.dot_general(ds, query(s, cols), TN, preferred_element_type=jnp.float32) * scale
        dk_ref[keys, cols] = dk.astype(jnp.bfloat16)
        give(tokens, s, cols.start, jnp.dot(ds, k_ref[keys, cols], preferred_element_type=jnp.float32) * scale)

    each = len(items) // PAIRS
    first, second = items[:each], items[each:]
    raw_a = [score(item) for item in first]
    raw_b = [score(item) for item in second]
    soft_a = [soften(*raw) for raw in raw_a]
    soft_b = []
    for i in range(each):
        value_side(first[i], soft_a[i][0])
        soft_b.append(soften(*raw_b[i]))
        key_side(first[i], soft_a[i][1])
    for i in range(each):
        value_side(second[i], soft_b[i][0])
        key_side(second[i], soft_b[i][1])
    dwv = jnp.dot(ft_ref[...], dv_ref[...], preferred_element_type=jnp.float32)
    keepv_ref[:128, :] = dwv[:128]
    keepv_ref[128:, :] = dwv[256:384]
    put(sendv_ref, jnp.concatenate([dwv[128:256], dwv[384:]], axis=0))
    put(sendk_ref, jnp.dot(ft_ref[256:, :], dk_ref[...], preferred_element_type=jnp.float32))
    keepk_ref[...] = jnp.dot(ft_ref[:256, :], dk_ref[...], preferred_element_type=jnp.float32)


def attend(coords, rows, queries, grad_out, oth, kv_weight):
    tokens, width = queries.shape
    steps = width // WIDE // NC
    half = FEAT // 2
    every = NC * WANT * ROWS
    queries, grad_out, kv_weight = (
        pltpu.with_memory_space_constraint(a, pltpu.HBM) for a in (queries, grad_out, kv_weight)
    )
    mine = lambda rows, at0: pl.BlockSpec((rows, WIDE), lambda h, at: (0, at0 + at[3] * steps + h))
    col = lambda rows: pl.BlockSpec((rows, WIDE), lambda h, at: (0, h))
    shape = lambda rows, dtype: jax.ShapeDtypeStruct((rows, width // NC), dtype)
    return pl.pallas_call(
        first_kernel,
        grid_spec=pltpu.PrefetchScalarGridSpec(
            num_scalar_prefetch=1,
            grid=(steps,),
            in_specs=[pl.BlockSpec(memory_space=pltpu.VMEM)] * 3
            + [mine(tokens, 0), mine(tokens, 0), col(2 * tokens), mine(FEAT, 0), mine(FEAT, NC * steps)],
            out_specs=[
                col(2 * tokens), col(2 * tokens),
                col(half), col(half + TILE_R), col(half), col(half + TILE_R),
            ],
            scratch_shapes=[
                pltpu.VMEM((NC * WANT, RB, TILE_R, FEAT), jnp.bfloat16),
                pltpu.VMEM((FEAT, every), jnp.bfloat16),
            ]
            + [pltpu.VMEM((every, WIDE), jnp.bfloat16)] * 4,
        ),
        out_shape=[
            shape(2 * tokens, jnp.bfloat16), shape(2 * tokens, jnp.bfloat16),
            shape(half, jnp.float32), shape(half + TILE_R, jnp.int16),
            shape(half, jnp.float32), shape(half + TILE_R, jnp.int16),
        ],
        compiler_params=pltpu.CompilerParams(vmem_limit_bytes=36 * 2**20),
        cost_estimate=pl.CostEstimate(flops=11 * 10**9, bytes_accessed=8 * 2**20, transcendentals=10**6),
        name="attend",
    )(coords, *rows, queries, grad_out, oth, kv_weight, kv_weight)


def fold_kernel(kept_ref, came_ref, keep_ref, send_ref):
    rows = keep_ref.shape[0]
    total = kept_ref[...] + decode(came_ref)
    put(send_ref, total[rows:])
    keep_ref[...] = total[:rows]


def split_kernel(*refs):
    sums, keep_ref, send_refs = refs[: 4 * PARTS], refs[4 * PARTS], refs[4 * PARTS + 1 :]
    rows, width = keep_ref.shape
    wide = width // (2 * PARTS)
    for i in range(2 * PARTS):
        cols = slice(i * wide, (i + 1) * wide)
        total = sums[2 * i][...] + decode(sums[2 * i + 1])
        coded, power = encode_rows(total[rows:])
        for p, ref in enumerate(send_refs):
            ref[:, cols] = coded[p * rows : (p + 1) * rows]
            ref[:, width + i * DH : width + (i + 1) * DH] = power[p * rows : (p + 1) * rows]
        keep_ref[:, cols] = total[:rows]


def join_kernel(kept_ref, *refs):
    rows, width = kept_ref.shape
    wide = width // (2 * PARTS)
    parts = []
    for i in range(2 * PARTS):
        cols = slice(i * wide, (i + 1) * wide)
        total = kept_ref[:, cols]
        for ref in refs[:-1]:
            total = total + decode_rows(ref[:, cols], ref[:, width + i * DH : width + (i + 1) * DH])
        parts.append(total)
    total = jnp.concatenate(parts, axis=1)
    rows, wide = rows // NZ, width // 4
    for z in range(NZ):
        mine = total[z * rows : (z + 1) * rows]
        mine = jnp.concatenate([mine[:, q * wide : (q + 1) * wide] for q in range(4)], axis=0)
        refs[-1][z, :, :wide], refs[-1][z, :, wide:] = encode_rows(mine)


def z_kernel(got_ref, out_ref):
    wide = got_ref.shape[2] - DH
    total = None
    for z in range(NZ):
        piece = decode_rows(got_ref[z, :, :wide], got_ref[z, :, wide:])
        total = piece if z == 0 else total + piece
    rows = out_ref.shape[0]
    for q in range(4):
        out_ref[:, q * wide : (q + 1) * wide] = total[q * rows : (q + 1) * rows]


def copy_all(copies):
    for cp in copies:
        cp.start()
    for cp in copies:
        cp.wait()


def halves_kernel(coords_ref, q_ref, g_ref, out_ref, sems):
    tokens, width = q_ref.shape
    at = pl.multiple_of((1 - coords_ref[3]) * (width // NC), width // NC)
    copy_all(
        [
            pltpu.make_async_copy(ref.at[:, pl.ds(at, width // NC)], out_ref.at[pl.ds(i * tokens, tokens)], sems.at[i])
            for i, ref in enumerate((q_ref, g_ref))
        ]
    )


def place_kernel(coords_ref, *refs):
    srcs, (att_ref, dq_ref, sems) = refs[: 2 * PARTS], refs[2 * PARTS :]
    tokens, width = att_ref.shape
    wide = width // NC // PARTS
    copies = []
    for i, src in enumerate(srcs):
        core = coords_ref[3] if i < PARTS else 1 - coords_ref[3]
        at = pl.multiple_of(core * (width // NC) + i % PARTS * wide, wide)
        for j, dst in enumerate((att_ref, dq_ref)):
            copies.append(
                pltpu.make_async_copy(
                    src.at[pl.ds(j * tokens, tokens)], dst.at[:, pl.ds(at, wide)], sems.at[2 * i + j]
                )
            )
    copy_all(copies)


def local(kernel, name, out_shape, *args, coords=None, copies=0):
    space = pl.BlockSpec(memory_space=pl.ANY if copies else pltpu.VMEM)
    smem = [] if coords is None else [pl.BlockSpec(memory_space=pltpu.SMEM)]
    return pl.pallas_call(
        kernel,
        in_specs=smem + [space] * len(args),
        out_specs=jax.tree.map(lambda _: space, out_shape),
        out_shape=out_shape,
        scratch_shapes=[pltpu.SemaphoreType.DMA((copies,))] if copies else [],
        compiler_params=pltpu.CompilerParams(vmem_limit_bytes=16 * 2**20),
        name=name,
    )(*([] if coords is None else [coords]), *args)


def fetch(coords, neighbour_ids, entry_home, cache):
    ents = cache.shape[0]
    vmem = pl.BlockSpec(memory_space=pltpu.VMEM)
    smem = pl.BlockSpec(memory_space=pltpu.SMEM)
    pieces = pl.pallas_call(
        spread_kernel,
        in_specs=[pl.BlockSpec(memory_space=pl.ANY)] * 4,
        out_specs=vmem,
        out_shape=jax.ShapeDtypeStruct((RB * FB, ents + 1, TILE_R, DH), jnp.bfloat16),
        scratch_shapes=[
            pltpu.SMEM(neighbour_ids.shape[::-1], jnp.int32),
            pltpu.SMEM(entry_home.shape, jnp.int32),
            pltpu.SemaphoreType.DMA((RB * FB + 2,)),
        ],
        compiler_params=pltpu.CompilerParams(vmem_limit_bytes=16 * 2**20),
        name="spread",
    )(
        coords,
        *(pltpu.with_memory_space_constraint(a, pltpu.HBM) for a in (neighbour_ids.T, entry_home, cache)),
    )
    store = lax.all_to_all(pieces, PLANE, split_axis=0, concat_axis=0, tiled=True)
    spots = store[:, ents, 0, :WANT].astype(jnp.int32)
    picked = pl.pallas_call(
        pick_kernel,
        in_specs=[smem, vmem],
        out_specs=vmem,
        out_shape=pltpu.VMEM((N_DB * WANT, TILE_R, DH), jnp.bfloat16),
        compiler_params=pltpu.CompilerParams(vmem_limit_bytes=16 * 2**20),
        name="pick",
    )(spots, store)
    picked, coords = lax.optimization_barrier((picked, coords))
    answer = lax.all_to_all(
        picked.reshape(N_DB, WANT, TILE_R, DH), PLANE, split_axis=0, concat_axis=0, tiled=True
    )
    return answer, coords


def hops(mask, second):
    out = []
    for y in range(NY):
        for x in range(NX):
            for c in range(NC):
                to = (y, x ^ mask) if c == second else (y ^ mask, x)
                out.append(((y * NX + x) * NC + c, (to[0] * NX + to[1]) * NC + c))
    return out


def body(queries, grad_out, neighbour_ids, entry_home, cache, kv_weight):
    coords = jnp.stack([lax.axis_index(axis).astype(jnp.int32) for axis in ALL])
    tokens, width = queries.shape
    shape = jax.ShapeDtypeStruct
    swap = lambda v: lax.ppermute(v, "core", [(0, 1), (1, 0)])
    answer, coords = fetch(coords, neighbour_ids, entry_home, cache)
    hbm = lambda v: pltpu.with_memory_space_constraint(v, pltpu.HBM)
    theirs = shape((2 * tokens, width // NC), queries.dtype)
    oth = swap(local(halves_kernel, "halves", theirs, hbm(queries), hbm(grad_out), coords=coords, copies=2))
    half, quarter = FEAT // 2, FEAT // 4
    wide = width // NC // PARTS
    folded = [shape((quarter, wide), jnp.float32), shape((quarter + TILE_R, wide), jnp.int16)]
    tie = lax.optimization_barrier

    def one(keep_k, send_k, keep_v, send_v):
        return [keep_k, lax.ppermute(send_k, PLANE, hops(1, 0)), keep_v, lax.ppermute(send_v, PLANE, hops(3, 0))]

    def two(keep_k, came_k, keep_v, came_v):
        out = []
        for kept, came, mask in ((keep_k, came_k, 3), (keep_v, came_v, 1)):
            kept, sent = local(fold_kernel, "fold", folded, kept, came)
            out += [kept, lax.ppermute(sent, PLANE, hops(mask, 0))]
        return out

    args = (queries, grad_out, oth, kv_weight)
    own, other, *grads = attend(coords, (answer, swap(answer[:16]), swap(answer[16:])), *args)
    sums = one(*grads)
    other = swap(other)
    sums = two(*sums)
    outs = [shape(queries.shape, queries.dtype)] * 2
    outs = local(place_kernel, "place", outs, own, other, coords=coords, copies=4)
    sums[3], outs = tie((sums[3], outs))
    part = quarter // 4
    shapes = [shape((part, width), jnp.float32)]
    shapes += [shape((part, width + 2 * PARTS * DH), jnp.int16)] * 3
    kept, *sent = local(split_kernel, "split", shapes, *sums)
    came = [lax.ppermute(v, PLANE, hops(mask, 1)) for v, mask in zip(sent, RING[1:])]
    pieces = local(join_kernel, "join", shape((NZ, 4 * part // NZ, width // 4 + DH), jnp.int16), kept, *came)
    got = lax.all_to_all(pieces, "z", split_axis=0, concat_axis=0, tiled=True)
    total = local(z_kernel, "zsum", shape((2 * NC, width), jnp.float32), got)
    core = lax.axis_index("core")
    mine = lax.dynamic_slice(total, (2 * core, 0), (2, width))
    came = swap(lax.dynamic_slice(total, (2 - 2 * core, 0), (2, width)))
    low, high = jnp.where(core == 0, mine, came), jnp.where(core == 0, came, mine)
    weight_grad = jnp.concatenate(
        [low[:, : width // 2], high[:, : width // 2], low[:, width // 2 :], high[:, width // 2 :]], axis=1
    )
    return (*outs, weight_grad)


def solution(mesh):
    grid = Mesh(mesh.devices.reshape(NZ, NY, NX, NC), ALL)
    return jax.shard_map(
        body,
        mesh=grid,
        in_specs=(P(ALL, None), P(ALL, None), P(ALL, None), P(), P(PLANE, None, None), P()),
        out_specs=(P(ALL, None), P(ALL, None), P(ALL, None)),
        check_vma=False,
    )
```

```python
import functools

import jax
import jax.numpy as jnp
from jax import lax
from jax.experimental import pallas as pl
from jax.experimental.pallas import tpu as pltpu
from jax.sharding import Mesh, PartitionSpec as P

DH = 128
STRETCH = 64
NZ, NY, NX, NC = 8, 4, 4, 2
N_DB = NY * NX * NC
KEYS = 256
ROWS = 128
FEAT = 512
WANT = 8
PAIR = 2 * DH
STEPS = 32000.0
PARTS = 1
PAIRS = 2
WIDE = PAIRS * PAIR
RING = (0, 3, 1, 2)
TILE_R = 16
RB = ROWS // TILE_R
FB = FEAT // DH
NT = (((1,), (1,)), ((), ()))
TN = (((0,), (0,)), ((), ()))
ALL = ("z", "y", "x", "core")
PLANE = ("y", "x", "core")


def spread_kernel(coords_ref, ids_hbm, home_hbm, cache_ref, out_ref, ids_ref, home_ref, sems):
    ents = cache_ref.shape[0]
    small = [
        pltpu.make_async_copy(ids_hbm, ids_ref, sems.at[RB * FB]),
        pltpu.make_async_copy(home_hbm, home_ref, sems.at[RB * FB + 1]),
    ]
    copies = []
    for rb in range(RB):
        for fb in range(FB):
            m = rb * FB + fb
            copies.append(
                pltpu.make_async_copy(
                    cache_ref.at[:, rb * TILE_R : (rb + 1) * TILE_R, fb * DH : (fb + 1) * DH],
                    out_ref.at[m, pl.ds(0, ents)],
                    sems.at[m],
                )
            )
    for cp in small + copies:
        cp.start()
    for cp in small:
        cp.wait()
    row = lax.broadcasted_iota(jnp.int32, (TILE_R, DH), 0)
    lane = lax.broadcasted_iota(jnp.int32, (TILE_R, DH), 1)
    tile = jnp.zeros((TILE_R, DH), jnp.float32)
    for k in range(WANT):
        spot = home_ref[ids_ref[k % 2, k // 2]].astype(jnp.float32)
        tile = jnp.where((row == 0) & (lane == k), spot, tile)
    tile = tile.astype(jnp.bfloat16)
    for m in range(RB * FB):
        out_ref[m, ents] = tile
    for cp in copies:
        cp.wait()


def pick_kernel(spots_ref, store_ref, out_ref):
    def one(d, carry):
        spots = [spots_ref[d, k] for k in range(WANT)]
        tiles = [store_ref[spot] for spot in spots]
        for k in range(WANT):
            out_ref[d * WANT + k] = tiles[k]
        return carry

    lax.fori_loop(0, out_ref.shape[0] // WANT, one, 0, unroll=8)


def encode(x):
    top = jnp.maximum(jnp.max(jnp.abs(x), axis=0, keepdims=True), 1e-36)
    power = jnp.ceil(jnp.log2(top))
    coded = jnp.round(x * jnp.exp2(-power) * STEPS).astype(jnp.int32)
    power = jnp.broadcast_to(power.astype(jnp.int32), (TILE_R, x.shape[1]))
    return coded.astype(jnp.int16), power.astype(jnp.int16)


def decode(ref):
    rows = ref.shape[0] - TILE_R
    power = ref[rows:, :].astype(jnp.int32)[:1].astype(jnp.float32)
    return ref[:rows, :].astype(jnp.int32).astype(jnp.float32) * (1.0 / STEPS) * jnp.exp2(power)


def put(ref, x):
    coded, power = encode(x)
    rows = ref.shape[0] - TILE_R
    ref[:rows, :] = coded
    ref[rows:, :] = power


def encode_rows(x):
    top = jnp.maximum(jnp.max(jnp.abs(x), axis=1, keepdims=True), 1e-36)
    power = jnp.ceil(jnp.log2(top))
    coded = jnp.round(x * jnp.exp2(-power) * STEPS).astype(jnp.int32)
    power = jnp.broadcast_to(power.astype(jnp.int32), (x.shape[0], DH))
    return coded.astype(jnp.int16), power.astype(jnp.int16)


def decode_rows(coded, power):
    power = power.astype(jnp.int32).astype(jnp.float32)[:, :1]
    return coded.astype(jnp.int32).astype(jnp.float32) * (1.0 / STEPS) * jnp.exp2(power)


def row_order(coords_ref):
    old = lax.broadcasted_iota(jnp.int32, (1, FEAT), 1)
    dx = ((old >> 2) & 3) ^ coords_ref[2]
    dy = ((old >> 4) & 3) ^ coords_ref[1]
    z = old >> 6
    px = jnp.where(dx == 3, 1, jnp.where(dx == 1, 2, jnp.where(dx == 2, 3, 0)))
    py = jnp.where(dy == 3, 1, jnp.where(dy == 1, 2, jnp.where(dy == 2, 3, 0)))
    core = coords_ref[3]
    first = jnp.where(core == 0, px, py)
    second = jnp.where(core == 0, py, px)
    place = first * 128 + second * 32 + z * 4 + (old & 3)
    new = lax.broadcasted_iota(jnp.int32, (FEAT, FEAT), 0)
    return jnp.where(new == place, 1.0, 0.0).astype(jnp.bfloat16)


def lay_rows(coords_ref, refs, f_ref, ft_ref):
    each = RB * FB // len(refs)
    for rb in range(RB):
        for fb in range(FB):
            m = rb * FB + fb
            for w in range(WANT):
                f_ref[w, rb, :, fb * DH : (fb + 1) * DH] = refs[m // each][m % each, w]
    f = f_ref[...].reshape(WANT * ROWS, FEAT)
    ft_ref[...] = lax.dot_general(row_order(coords_ref), f, NT, preferred_element_type=jnp.float32).astype(
        jnp.bfloat16
    )


def project(f_ref, wk_ref, wv_ref, k_ref, v_ref):
    f = f_ref[...].reshape(WANT * ROWS, FEAT)
    k_ref[...] = jnp.dot(f, wk_ref[...], preferred_element_type=jnp.float32).astype(jnp.bfloat16)
    v_ref[...] = jnp.dot(f, wv_ref[...], preferred_element_type=jnp.float32).astype(jnp.bfloat16)


def own_kernel(coords_ref, r_ref, f_ref, ft_ref):
    lay_rows(coords_ref, (r_ref,), f_ref, ft_ref)


def attend_kernel(
    coords_ref, rr0_ref, rr1_ref, f0_ref, ft0_ref, q_ref, g_ref, qg_ref, wk_ref, wv_ref,
    own_ref, oth_ref, keepk_ref, sendk_ref, keepv_ref, sendv_ref,
    f1_ref, ft1_ref, k0_ref, v0_ref, k1_ref, v1_ref, dk_ref, dv_ref,
):
    scale = DH ** (-0.5)
    tokens = q_ref.shape[0]
    near = WANT * ROWS

    @pl.when(pl.program_id(0) == 0)
    def _():
        lay_rows(coords_ref, (rr0_ref, rr1_ref), f1_ref, ft1_ref)

    project(f0_ref, wk_ref, wv_ref, k0_ref, v0_ref)
    project(f1_ref, wk_ref, wv_ref, k1_ref, v1_ref)

    def held(refs, keys, cols):
        ref, at = (refs[0], keys.start) if keys.start < near else (refs[1], keys.start - near)
        return ref[at : at + KEYS, cols]

    keyed = functools.partial(held, (k0_ref, k1_ref))
    valued = functools.partial(held, (v0_ref, v1_ref))

    def weight(rows, grad_ref):
        return jnp.dot(ft0_ref[rows, :], grad_ref[:near, :], preferred_element_type=jnp.float32) + jnp.dot(
            ft1_ref[rows, :], grad_ref[near:, :], preferred_element_type=jnp.float32
        )

    left = lax.broadcasted_iota(jnp.int32, (STRETCH, PAIR), 1) < DH
    zero = jnp.zeros((STRETCH, PAIR), jnp.bfloat16)
    def both(t):
        return jnp.concatenate([jnp.where(left, t, zero), jnp.where(left, zero, t)], axis=0)

    def query(s, cols):
        at = s * STRETCH
        ref, at = (q_ref, at) if at < tokens else (qg_ref, at - tokens)
        return both(ref[at : at + STRETCH, cols])

    def grad(s, cols):
        at = s * STRETCH
        ref = g_ref if at < tokens else qg_ref
        return both(ref[at : at + STRETCH, cols])

    def give(base, s, at_col, x):
        at = s * STRETCH
        ref, at = (own_ref, at) if at < tokens else (oth_ref, at - tokens)
        rows = slice(base + at, base + at + STRETCH)
        ref[rows, at_col : at_col + DH] = x[:STRETCH, :DH].astype(jnp.bfloat16)
        ref[rows, at_col + DH : at_col + PAIR] = x[STRETCH:, DH:].astype(jnp.bfloat16)

    items = [
        (s, slice(s * KEYS, (s + 1) * KEYS), slice(p * PAIR, (p + 1) * PAIR))
        for p in range(PAIRS)
        for s in range(NC * tokens // STRETCH)
    ]
    scores, dprob, pbs, ds = [], [], [], []
    for s, keys, cols in items:
        scores.append(
            lax.dot_general(keyed(keys, cols), query(s, cols), NT, preferred_element_type=jnp.float32) * scale
        )
        dprob.append(lax.dot_general(valued(keys, cols), grad(s, cols), NT, preferred_element_type=jnp.float32))
    for x, dp in zip(scores, dprob):
        expo = jnp.exp(x - jnp.max(x, axis=0, keepdims=True))
        probs = expo * (1.0 / jnp.sum(expo, axis=0, keepdims=True))
        pb = probs.astype(jnp.bfloat16)
        delta = jnp.sum(pb.astype(jnp.float32) * dp, axis=0, keepdims=True)
        pbs.append(pb)
        ds.append((probs * (dp - delta)).astype(jnp.bfloat16))
    for i, (s, keys, cols) in enumerate(items):
        dv_ref[keys, cols] = jnp.dot(pbs[i], grad(s, cols), preferred_element_type=jnp.float32).astype(jnp.bfloat16)
        ctx = lax.dot_general(pbs[i], valued(keys, cols), TN, preferred_element_type=jnp.float32)
        give(0, s, cols.start, ctx)
    for i, (s, keys, cols) in enumerate(items):
        dk_ref[keys, cols] = (
            jnp.dot(ds[i], query(s, cols), preferred_element_type=jnp.float32) * scale
        ).astype(jnp.bfloat16)
        dq = lax.dot_general(ds[i], keyed(keys, cols), TN, preferred_element_type=jnp.float32) * scale
        give(tokens, s, cols.start, dq)
    dwv = weight(slice(None), dv_ref)
    keepv_ref[:128, :] = dwv[:128]
    keepv_ref[128:, :] = dwv[256:384]
    put(sendv_ref, jnp.concatenate([dwv[128:256], dwv[384:]], axis=0))
    put(sendk_ref, weight(slice(256, None), dk_ref))
    keepk_ref[...] = weight(slice(0, 256), dk_ref)


def weight_specs(width):
    steps = width // WIDE // NC
    return [
        pl.BlockSpec((FEAT, WIDE), lambda h, at, skip=skip: (0, skip + at[3] * steps + h)) for skip in (0, NC * steps)
    ]


def attend(coords, rows, f0, ft0, queries, grad_out, oth, kv_weight):
    tokens, width = queries.shape
    steps = width // WIDE // NC
    half = FEAT // 2
    near = WANT * ROWS
    queries, grad_out, kv_weight = (
        pltpu.with_memory_space_constraint(a, pltpu.HBM) for a in (queries, grad_out, kv_weight)
    )
    vmem = pl.BlockSpec(memory_space=pltpu.VMEM)
    mine = pl.BlockSpec((tokens, WIDE), lambda h, at: (0, at[3] * steps + h))
    col = lambda rows: pl.BlockSpec((rows, WIDE), lambda h, at: (0, h))
    shape = lambda rows, dtype: jax.ShapeDtypeStruct((rows, width // NC), dtype)
    return pl.pallas_call(
        attend_kernel,
        grid_spec=pltpu.PrefetchScalarGridSpec(
            num_scalar_prefetch=1,
            grid=(steps,),
            in_specs=[vmem] * 4 + [mine, mine, col(2 * tokens)] + weight_specs(width),
            out_specs=[
                col(2 * tokens), col(2 * tokens),
                col(half), col(half + TILE_R), col(half), col(half + TILE_R),
            ],
            scratch_shapes=[
                pltpu.VMEM((WANT, RB, TILE_R, FEAT), jnp.bfloat16),
                pltpu.VMEM((FEAT, near), jnp.bfloat16),
            ]
            + [pltpu.VMEM((near, WIDE), jnp.bfloat16)] * 4
            + [pltpu.VMEM((NC * near, WIDE), jnp.bfloat16)] * 2,
        ),
        out_shape=[
            shape(2 * tokens, jnp.bfloat16), shape(2 * tokens, jnp.bfloat16),
            shape(half, jnp.float32), shape(half + TILE_R, jnp.int16),
            shape(half, jnp.float32), shape(half + TILE_R, jnp.int16),
        ],
        compiler_params=pltpu.CompilerParams(vmem_limit_bytes=36 * 2**20),
        cost_estimate=pl.CostEstimate(flops=9 * 10**9, bytes_accessed=8 * 2**20, transcendentals=10**6),
        name="attend",
    )(coords, *rows, f0, ft0, queries, grad_out, oth, kv_weight, kv_weight)


def fold_kernel(kept_ref, came_ref, keep_ref, send_ref):
    rows = keep_ref.shape[0]
    total = kept_ref[...] + decode(came_ref)
    put(send_ref, total[rows:])
    keep_ref[...] = total[:rows]


def split_kernel(*refs):
    sums, keep_ref, send_refs = refs[: 4 * PARTS], refs[4 * PARTS], refs[4 * PARTS + 1 :]
    rows, width = keep_ref.shape
    wide = width // (2 * PARTS)
    for i in range(2 * PARTS):
        cols = slice(i * wide, (i + 1) * wide)
        total = sums[2 * i][...] + decode(sums[2 * i + 1])
        coded, power = encode_rows(total[rows:])
        for p, ref in enumerate(send_refs):
            ref[:, cols] = coded[p * rows : (p + 1) * rows]
            ref[:, width + i * DH : width + (i + 1) * DH] = power[p * rows : (p + 1) * rows]
        keep_ref[:, cols] = total[:rows]


def join_kernel(kept_ref, *refs):
    rows, width = kept_ref.shape
    wide = width // (2 * PARTS)
    parts = []
    for i in range(2 * PARTS):
        cols = slice(i * wide, (i + 1) * wide)
        total = kept_ref[:, cols]
        for ref in refs[:-1]:
            total = total + decode_rows(ref[:, cols], ref[:, width + i * DH : width + (i + 1) * DH])
        parts.append(total)
    total = jnp.concatenate(parts, axis=1)
    rows, wide = rows // NZ, width // 4
    for z in range(NZ):
        mine = total[z * rows : (z + 1) * rows]
        mine = jnp.concatenate([mine[:, q * wide : (q + 1) * wide] for q in range(4)], axis=0)
        refs[-1][z, :, :wide], refs[-1][z, :, wide:] = encode_rows(mine)


def z_kernel(got_ref, out_ref):
    wide = got_ref.shape[2] - DH
    total = None
    for z in range(NZ):
        piece = decode_rows(got_ref[z, :, :wide], got_ref[z, :, wide:])
        total = piece if z == 0 else total + piece
    rows = out_ref.shape[0]
    for q in range(4):
        out_ref[:, q * wide : (q + 1) * wide] = total[q * rows : (q + 1) * rows]


def copy_all(copies):
    for cp in copies:
        cp.start()
    for cp in copies:
        cp.wait()


def halves_kernel(coords_ref, q_ref, g_ref, out_ref, sems):
    tokens, width = q_ref.shape
    at = pl.multiple_of((1 - coords_ref[3]) * (width // NC), width // NC)
    copy_all(
        [
            pltpu.make_async_copy(ref.at[:, pl.ds(at, width // NC)], out_ref.at[pl.ds(i * tokens, tokens)], sems.at[i])
            for i, ref in enumerate((q_ref, g_ref))
        ]
    )


def place_kernel(coords_ref, *refs):
    srcs, (att_ref, dq_ref, sems) = refs[: 2 * PARTS], refs[2 * PARTS :]
    tokens, width = att_ref.shape
    wide = width // NC // PARTS
    copies = []
    for i, src in enumerate(srcs):
        core = coords_ref[3] if i < PARTS else 1 - coords_ref[3]
        at = pl.multiple_of(core * (width // NC) + i % PARTS * wide, wide)
        for j, dst in enumerate((att_ref, dq_ref)):
            copies.append(
                pltpu.make_async_copy(
                    src.at[pl.ds(j * tokens, tokens)], dst.at[:, pl.ds(at, wide)], sems.at[2 * i + j]
                )
            )
    copy_all(copies)


def local(kernel, name, out_shape, *args, coords=None, copies=0):
    space = pl.BlockSpec(memory_space=pl.ANY if copies else pltpu.VMEM)
    smem = [] if coords is None else [pl.BlockSpec(memory_space=pltpu.SMEM)]
    return pl.pallas_call(
        kernel,
        in_specs=smem + [space] * len(args),
        out_specs=jax.tree.map(lambda _: space, out_shape),
        out_shape=out_shape,
        scratch_shapes=[pltpu.SemaphoreType.DMA((copies,))] if copies else [],
        compiler_params=pltpu.CompilerParams(vmem_limit_bytes=16 * 2**20),
        name=name,
    )(*([] if coords is None else [coords]), *args)


def fetch(coords, neighbour_ids, entry_home, cache):
    ents = cache.shape[0]
    vmem = pl.BlockSpec(memory_space=pltpu.VMEM)
    smem = pl.BlockSpec(memory_space=pltpu.SMEM)
    pieces = pl.pallas_call(
        spread_kernel,
        in_specs=[pl.BlockSpec(memory_space=pl.ANY)] * 4,
        out_specs=vmem,
        out_shape=jax.ShapeDtypeStruct((RB * FB, ents + 1, TILE_R, DH), jnp.bfloat16),
        scratch_shapes=[
            pltpu.SMEM(neighbour_ids.shape[::-1], jnp.int32),
            pltpu.SMEM(entry_home.shape, jnp.int32),
            pltpu.SemaphoreType.DMA((RB * FB + 2,)),
        ],
        compiler_params=pltpu.CompilerParams(vmem_limit_bytes=16 * 2**20),
        name="spread",
    )(
        coords,
        *(pltpu.with_memory_space_constraint(a, pltpu.HBM) for a in (neighbour_ids.T, entry_home, cache)),
    )
    store = lax.all_to_all(pieces, PLANE, split_axis=0, concat_axis=0, tiled=True)
    spots = store[:, ents, 0, :WANT].astype(jnp.int32)
    spots = spots + (spots >> 3)
    store = store.reshape(N_DB * (ents + 1), TILE_R, DH)
    picked = pl.pallas_call(
        pick_kernel,
        in_specs=[smem, vmem],
        out_specs=vmem,
        out_shape=pltpu.VMEM((N_DB * WANT, TILE_R, DH), jnp.bfloat16),
        compiler_params=pltpu.CompilerParams(vmem_limit_bytes=16 * 2**20),
        name="pick",
    )(spots, store)
    picked, coords = lax.optimization_barrier((picked, coords))
    answer = lax.all_to_all(
        picked.reshape(N_DB, WANT, TILE_R, DH), PLANE, split_axis=0, concat_axis=0, tiled=True
    )
    return answer, coords


def hops(mask, second):
    out = []
    for y in range(NY):
        for x in range(NX):
            for c in range(NC):
                to = (y, x ^ mask) if c == second else (y ^ mask, x)
                out.append(((y * NX + x) * NC + c, (to[0] * NX + to[1]) * NC + c))
    return out


def body(queries, grad_out, neighbour_ids, entry_home, cache, kv_weight):
    coords = jnp.stack([lax.axis_index(axis).astype(jnp.int32) for axis in ALL])
    tokens, width = queries.shape
    shape = jax.ShapeDtypeStruct
    swap = lambda v: lax.ppermute(v, "core", [(0, 1), (1, 0)])
    answer, coords = fetch(coords, neighbour_ids, entry_home, cache)
    hbm = lambda v: pltpu.with_memory_space_constraint(v, pltpu.HBM)
    theirs = shape((2 * tokens, width // NC), queries.dtype)
    oth = swap(local(halves_kernel, "halves", theirs, hbm(queries), hbm(grad_out), coords=coords, copies=2))
    half, quarter = FEAT // 2, FEAT // 4
    wide = width // NC // PARTS
    folded = [shape((quarter, wide), jnp.float32), shape((quarter + TILE_R, wide), jnp.int16)]
    tie = lax.optimization_barrier

    def one(keep_k, send_k, keep_v, send_v):
        return [keep_k, lax.ppermute(send_k, PLANE, hops(1, 0)), keep_v, lax.ppermute(send_v, PLANE, hops(3, 0))]

    def two(keep_k, came_k, keep_v, came_v):
        out = []
        for kept, came, mask in ((keep_k, came_k, 3), (keep_v, came_v, 1)):
            kept, sent = local(fold_kernel, "fold", folded, kept, came)
            out += [kept, lax.ppermute(sent, PLANE, hops(mask, 0))]
        return out

    args = (queries, grad_out, oth, kv_weight)
    rows = (swap(answer[:16]), swap(answer[16:]))
    laid = [pltpu.VMEM((WANT, RB, TILE_R, FEAT), jnp.bfloat16), pltpu.VMEM((FEAT, WANT * ROWS), jnp.bfloat16)]
    laid = local(own_kernel, "own_side", laid, answer, coords=coords)
    rows, laid = tie((rows, laid))
    own, other, *grads = attend(coords, rows, *laid, *args)
    sums = one(*grads)
    other = swap(other)
    sums = two(*sums)
    outs = [shape(queries.shape, queries.dtype)] * 2
    outs = local(place_kernel, "place", outs, own, other, coords=coords, copies=4)
    sums[3], outs = tie((sums[3], outs))
    part = quarter // 4
    shapes = [shape((part, width), jnp.float32)]
    shapes += [shape((part, width + 2 * PARTS * DH), jnp.int16)] * 3
    kept, *sent = local(split_kernel, "split", shapes, *sums)
    came = [lax.ppermute(v, PLANE, hops(mask, 1)) for v, mask in zip(sent, RING[1:])]
    pieces = local(join_kernel, "join", shape((NZ, 4 * part // NZ, width // 4 + DH), jnp.int16), kept, *came)
    got = lax.all_to_all(pieces, "z", split_axis=0, concat_axis=0, tiled=True)
    total = local(z_kernel, "zsum", shape((2 * NC, width), jnp.float32), got)
    core = lax.axis_index("core")
    mine = lax.dynamic_slice(total, (2 * core, 0), (2, width))
    came = swap(lax.dynamic_slice(total, (2 - 2 * core, 0), (2, width)))
    low, high = jnp.where(core == 0, mine, came), jnp.where(core == 0, came, mine)
    weight_grad = jnp.concatenate(
        [low[:, : width // 2], high[:, : width // 2], low[:, width // 2 :], high[:, width // 2 :]], axis=1
    )
    return (*outs, weight_grad)


def solution(mesh):
    grid = Mesh(mesh.devices.reshape(NZ, NY, NX, NC), ALL)
    return jax.shard_map(
        body,
        mesh=grid,
        in_specs=(P(ALL, None), P(ALL, None), P(ALL, None), P(), P(PLANE, None, None), P()),
        out_specs=(P(ALL, None), P(ALL, None), P(ALL, None)),
        check_vma=False,
    )
```

```python
import functools

import jax
import jax.numpy as jnp
from jax import lax
from jax.experimental import pallas as pl
from jax.experimental.pallas import tpu as pltpu
from jax.sharding import Mesh, PartitionSpec as P

DH = 128
STRETCH = 64
NZ, NY, NX, NC = 8, 4, 4, 2
N_DB = NY * NX * NC
KEYS = 256
ROWS = 128
FEAT = 512
WANT = 8
PAIR = 2 * DH
STEPS = 32000.0
PARTS = 1
PAIRS = 2
WIDE = PAIRS * PAIR
RING = (0, 3, 1, 2)
TILE_R = 16
RB = ROWS // TILE_R
FB = FEAT // DH
NT = (((1,), (1,)), ((), ()))
TN = (((0,), (0,)), ((), ()))
ALL = ("z", "y", "x", "core")
PLANE = ("y", "x", "core")


def spread_kernel(coords_ref, ids_hbm, home_hbm, cache_ref, out_ref, ids_ref, home_ref, sems):
    ents = cache_ref.shape[0]
    small = [
        pltpu.make_async_copy(ids_hbm, ids_ref, sems.at[RB * FB]),
        pltpu.make_async_copy(home_hbm, home_ref, sems.at[RB * FB + 1]),
    ]
    copies = []
    for rb in range(RB):
        for fb in range(FB):
            m = rb * FB + fb
            copies.append(
                pltpu.make_async_copy(
                    cache_ref.at[:, rb * TILE_R : (rb + 1) * TILE_R, fb * DH : (fb + 1) * DH],
                    out_ref.at[m, pl.ds(0, ents)],
                    sems.at[m],
                )
            )
    for cp in small + copies:
        cp.start()
    for cp in small:
        cp.wait()
    row = lax.broadcasted_iota(jnp.int32, (TILE_R, DH), 0)
    lane = lax.broadcasted_iota(jnp.int32, (TILE_R, DH), 1)
    tile = jnp.zeros((TILE_R, DH), jnp.float32)
    for k in range(WANT):
        spot = home_ref[ids_ref[k % 2, k // 2]].astype(jnp.float32)
        tile = jnp.where((row == 0) & (lane == k), spot, tile)
    tile = tile.astype(jnp.bfloat16)
    for m in range(RB * FB):
        out_ref[m, ents] = tile
    for cp in copies:
        cp.wait()


def pick_kernel(spots_ref, store_ref, out_ref):
    def one(d, carry):
        spots = [spots_ref[d, k] for k in range(WANT)]
        tiles = [store_ref[spot] for spot in spots]
        for k in range(WANT):
            out_ref[d * WANT + k] = tiles[k]
        return carry

    lax.fori_loop(0, out_ref.shape[0] // WANT, one, 0, unroll=8)


def encode(x):
    top = jnp.maximum(jnp.max(jnp.abs(x), axis=0, keepdims=True), 1e-36)
    power = jnp.ceil(jnp.log2(top))
    coded = jnp.round(x * jnp.exp2(-power) * STEPS).astype(jnp.int32)
    power = jnp.broadcast_to(power.astype(jnp.int32), (TILE_R, x.shape[1]))
    return coded.astype(jnp.int16), power.astype(jnp.int16)


def decode(ref):
    rows = ref.shape[0] - TILE_R
    power = ref[rows:, :].astype(jnp.int32)[:1].astype(jnp.float32)
    return ref[:rows, :].astype(jnp.int32).astype(jnp.float32) * (1.0 / STEPS) * jnp.exp2(power)


def put(ref, x):
    coded, power = encode(x)
    rows = ref.shape[0] - TILE_R
    ref[:rows, :] = coded
    ref[rows:, :] = power


def encode_rows(x):
    top = jnp.maximum(jnp.max(jnp.abs(x), axis=1, keepdims=True), 1e-36)
    power = jnp.ceil(jnp.log2(top))
    coded = jnp.round(x * jnp.exp2(-power) * STEPS).astype(jnp.int32)
    power = jnp.broadcast_to(power.astype(jnp.int32), (x.shape[0], DH))
    return coded.astype(jnp.int16), power.astype(jnp.int16)


def decode_rows(coded, power):
    power = power.astype(jnp.int32).astype(jnp.float32)[:, :1]
    return coded.astype(jnp.int32).astype(jnp.float32) * (1.0 / STEPS) * jnp.exp2(power)


def row_order(coords_ref):
    old = lax.broadcasted_iota(jnp.int32, (1, FEAT), 1)
    dx = ((old >> 2) & 3) ^ coords_ref[2]
    dy = ((old >> 4) & 3) ^ coords_ref[1]
    z = old >> 6
    px = jnp.where(dx == 3, 1, jnp.where(dx == 1, 2, jnp.where(dx == 2, 3, 0)))
    py = jnp.where(dy == 3, 1, jnp.where(dy == 1, 2, jnp.where(dy == 2, 3, 0)))
    core = coords_ref[3]
    first = jnp.where(core == 0, px, py)
    second = jnp.where(core == 0, py, px)
    place = first * 128 + second * 32 + z * 4 + (old & 3)
    new = lax.broadcasted_iota(jnp.int32, (FEAT, FEAT), 0)
    return jnp.where(new == place, 1.0, 0.0).astype(jnp.bfloat16)


def lay_rows(coords_ref, refs, f_ref, ft_ref):
    each = RB * FB // len(refs)
    for rb in range(RB):
        for fb in range(FB):
            m = rb * FB + fb
            for w in range(WANT):
                f_ref[w, rb, :, fb * DH : (fb + 1) * DH] = refs[m // each][m % each, w]
    f = f_ref[...].reshape(WANT * ROWS, FEAT)
    ft_ref[...] = lax.dot_general(row_order(coords_ref), f, NT, preferred_element_type=jnp.float32).astype(
        jnp.bfloat16
    )


def project(f_ref, wk_ref, wv_ref, k_ref, v_ref):
    f = f_ref[...].reshape(WANT * ROWS, FEAT)
    k_ref[...] = jnp.dot(f, wk_ref[...], preferred_element_type=jnp.float32).astype(jnp.bfloat16)
    v_ref[...] = jnp.dot(f, wv_ref[...], preferred_element_type=jnp.float32).astype(jnp.bfloat16)


def own_kernel(coords_ref, r_ref, f_ref, ft_ref):
    lay_rows(coords_ref, (r_ref,), f_ref, ft_ref)


def attend_kernel(
    coords_ref, rr0_ref, rr1_ref, f0_ref, ft0_ref, q_ref, g_ref, qg_ref, wk_ref, wv_ref,
    own_ref, oth_ref, keepk_ref, sendk_ref, keepv_ref, sendv_ref,
    f1_ref, ft1_ref, k0_ref, v0_ref, k1_ref, v1_ref, dk_ref, dv_ref,
):
    scale = DH ** (-0.5)
    tokens = q_ref.shape[0]
    near = WANT * ROWS

    @pl.when(pl.program_id(0) == 0)
    def _():
        lay_rows(coords_ref, (rr0_ref, rr1_ref), f1_ref, ft1_ref)

    project(f0_ref, wk_ref, wv_ref, k0_ref, v0_ref)
    project(f1_ref, wk_ref, wv_ref, k1_ref, v1_ref)

    def held(refs, keys, cols):
        ref, at = (refs[0], keys.start) if keys.start < near else (refs[1], keys.start - near)
        return ref[at : at + KEYS, cols]

    keyed = functools.partial(held, (k0_ref, k1_ref))
    valued = functools.partial(held, (v0_ref, v1_ref))

    def weight(rows, grad_ref):
        return jnp.dot(ft0_ref[rows, :], grad_ref[:near, :], preferred_element_type=jnp.float32) + jnp.dot(
            ft1_ref[rows, :], grad_ref[near:, :], preferred_element_type=jnp.float32
        )

    left = lax.broadcasted_iota(jnp.int32, (STRETCH, PAIR), 1) < DH
    zero = jnp.zeros((STRETCH, PAIR), jnp.bfloat16)
    def both(t):
        return jnp.concatenate([jnp.where(left, t, zero), jnp.where(left, zero, t)], axis=0)

    def query(s, cols):
        at = s * STRETCH
        ref, at = (q_ref, at) if at < tokens else (qg_ref, at - tokens)
        return both(ref[at : at + STRETCH, cols])

    def grad(s, cols):
        at = s * STRETCH
        ref = g_ref if at < tokens else qg_ref
        return both(ref[at : at + STRETCH, cols])

    def give(base, s, at_col, x):
        at = s * STRETCH
        ref, at = (own_ref, at) if at < tokens else (oth_ref, at - tokens)
        rows = slice(base + at, base + at + STRETCH)
        ref[rows, at_col : at_col + DH] = x[:STRETCH, :DH].astype(jnp.bfloat16)
        ref[rows, at_col + DH : at_col + PAIR] = x[STRETCH:, DH:].astype(jnp.bfloat16)

    items = [
        (s, slice(s * KEYS, (s + 1) * KEYS), slice(p * PAIR, (p + 1) * PAIR))
        for p in range(PAIRS)
        for s in range(NC * tokens // STRETCH)
    ]
    scores, dprob, pbs, ds = [], [], [], []
    for s, keys, cols in items:
        scores.append(
            lax.dot_general(keyed(keys, cols), query(s, cols), NT, preferred_element_type=jnp.float32) * scale
        )
        dprob.append(lax.dot_general(valued(keys, cols), grad(s, cols), NT, preferred_element_type=jnp.float32))
    for x, dp in zip(scores, dprob):
        expo = jnp.exp(x - jnp.max(x, axis=0, keepdims=True))
        probs = expo * (1.0 / jnp.sum(expo, axis=0, keepdims=True))
        pb = probs.astype(jnp.bfloat16)
        delta = jnp.sum(pb.astype(jnp.float32) * dp, axis=0, keepdims=True)
        pbs.append(pb)
        ds.append((probs * (dp - delta)).astype(jnp.bfloat16))
    for i, (s, keys, cols) in enumerate(items):
        dv_ref[keys, cols] = jnp.dot(pbs[i], grad(s, cols), preferred_element_type=jnp.float32).astype(jnp.bfloat16)
        ctx = lax.dot_general(pbs[i], valued(keys, cols), TN, preferred_element_type=jnp.float32)
        give(0, s, cols.start, ctx)
    for i, (s, keys, cols) in enumerate(items):
        dk_ref[keys, cols] = (
            jnp.dot(ds[i], query(s, cols), preferred_element_type=jnp.float32) * scale
        ).astype(jnp.bfloat16)
        dq = lax.dot_general(ds[i], keyed(keys, cols), TN, preferred_element_type=jnp.float32) * scale
        give(tokens, s, cols.start, dq)
    dwv = weight(slice(None), dv_ref)
    keepv_ref[:128, :] = dwv[:128]
    keepv_ref[128:, :] = dwv[256:384]
    put(sendv_ref, jnp.concatenate([dwv[128:256], dwv[384:]], axis=0))
    put(sendk_ref, weight(slice(256, None), dk_ref))
    keepk_ref[...] = weight(slice(0, 256), dk_ref)


def weight_specs(width):
    steps = width // WIDE // NC
    return [
        pl.BlockSpec((FEAT, WIDE), lambda h, at, skip=skip: (0, skip + at[3] * steps + h)) for skip in (0, NC * steps)
    ]


def attend(coords, rows, f0, ft0, queries, grad_out, oth, kv_weight):
    tokens, width = queries.shape
    steps = width // WIDE // NC
    half = FEAT // 2
    near = WANT * ROWS
    queries, grad_out, kv_weight = (
        pltpu.with_memory_space_constraint(a, pltpu.HBM) for a in (queries, grad_out, kv_weight)
    )
    vmem = pl.BlockSpec(memory_space=pltpu.VMEM)
    mine = pl.BlockSpec((tokens, WIDE), lambda h, at: (0, at[3] * steps + h))
    col = lambda rows: pl.BlockSpec((rows, WIDE), lambda h, at: (0, h))
    shape = lambda rows, dtype: jax.ShapeDtypeStruct((rows, width // NC), dtype)
    return pl.pallas_call(
        attend_kernel,
        grid_spec=pltpu.PrefetchScalarGridSpec(
            num_scalar_prefetch=1,
            grid=(steps,),
            in_specs=[vmem] * 4 + [mine, mine, col(2 * tokens)] + weight_specs(width),
            out_specs=[
                col(2 * tokens), col(2 * tokens),
                col(half), col(half + TILE_R), col(half), col(half + TILE_R),
            ],
            scratch_shapes=[
                pltpu.VMEM((WANT, RB, TILE_R, FEAT), jnp.bfloat16),
                pltpu.VMEM((FEAT, near), jnp.bfloat16),
            ]
            + [pltpu.VMEM((near, WIDE), jnp.bfloat16)] * 4
            + [pltpu.VMEM((NC * near, WIDE), jnp.bfloat16)] * 2,
        ),
        out_shape=[
            shape(2 * tokens, jnp.bfloat16), shape(2 * tokens, jnp.bfloat16),
            shape(half, jnp.float32), shape(half + TILE_R, jnp.int16),
            shape(half, jnp.float32), shape(half + TILE_R, jnp.int16),
        ],
        compiler_params=pltpu.CompilerParams(vmem_limit_bytes=36 * 2**20),
        cost_estimate=pl.CostEstimate(flops=9 * 10**9, bytes_accessed=8 * 2**20, transcendentals=10**6),
        name="attend",
    )(coords, *rows, f0, ft0, queries, grad_out, oth, kv_weight, kv_weight)


def fold_kernel(kept_ref, came_ref, keep_ref, send_ref):
    rows = keep_ref.shape[0]
    total = kept_ref[...] + decode(came_ref)
    put(send_ref, total[rows:])
    keep_ref[...] = total[:rows]


def split_kernel(*refs):
    sums, keep_ref, send_refs = refs[: 4 * PARTS], refs[4 * PARTS], refs[4 * PARTS + 1 :]
    rows, width = keep_ref.shape
    wide = width // (2 * PARTS)
    for i in range(2 * PARTS):
        cols = slice(i * wide, (i + 1) * wide)
        total = sums[2 * i][...] + decode(sums[2 * i + 1])
        coded, power = encode_rows(total[rows:])
        for p, ref in enumerate(send_refs):
            ref[:, cols] = coded[p * rows : (p + 1) * rows]
            ref[:, width + i * DH : width + (i + 1) * DH] = power[p * rows : (p + 1) * rows]
        keep_ref[:, cols] = total[:rows]


def join_kernel(kept_ref, *refs):
    rows, width = kept_ref.shape
    wide = width // (2 * PARTS)
    parts = []
    for i in range(2 * PARTS):
        cols = slice(i * wide, (i + 1) * wide)
        total = kept_ref[:, cols]
        for ref in refs[:-1]:
            total = total + decode_rows(ref[:, cols], ref[:, width + i * DH : width + (i + 1) * DH])
        parts.append(total)
    total = jnp.concatenate(parts, axis=1)
    rows, wide = rows // NZ, width // 4
    for z in range(NZ):
        mine = total[z * rows : (z + 1) * rows]
        mine = jnp.concatenate([mine[:, q * wide : (q + 1) * wide] for q in range(4)], axis=0)
        refs[-1][z, :, :wide], refs[-1][z, :, wide:] = encode_rows(mine)


def z_kernel(coords_ref, got_ref, mine_ref, away_ref):
    wide = got_ref.shape[2] - DH
    total = None
    for z in range(NZ):
        piece = decode_rows(got_ref[z, :, :wide], got_ref[z, :, wide:])
        total = piece if z == 0 else total + piece
    first = coords_ref[3] == 0
    for q in range(4):
        cols = slice(q * wide, (q + 1) * wide)
        low, high = total[4 * q : 4 * q + 2], total[4 * q + 2 : 4 * q + 4]
        mine_ref[:, cols] = jnp.where(first, low, high)
        away_ref[:, cols] = jnp.where(first, high, low)


def last_kernel(coords_ref, mine_ref, came_ref, out_ref):
    first = coords_ref[3] == 0
    width = mine_ref.shape[1] // 2
    low = jnp.where(first, mine_ref[...], came_ref[...])
    high = jnp.where(first, came_ref[...], mine_ref[...])
    for kv in range(2):
        for c, half in enumerate((low, high)):
            at = (kv * NC + c) * width
            out_ref[:, at : at + width] = half[:, kv * width : (kv + 1) * width]


def copy_all(copies):
    for cp in copies:
        cp.start()
    for cp in copies:
        cp.wait()


def halves_kernel(coords_ref, q_ref, g_ref, out_ref, sems):
    tokens, width = q_ref.shape
    at = pl.multiple_of((1 - coords_ref[3]) * (width // NC), width // NC)
    copy_all(
        [
            pltpu.make_async_copy(ref.at[:, pl.ds(at, width // NC)], out_ref.at[pl.ds(i * tokens, tokens)], sems.at[i])
            for i, ref in enumerate((q_ref, g_ref))
        ]
    )


def place_kernel(coords_ref, *refs):
    srcs, (att_ref, dq_ref, sems) = refs[: 2 * PARTS], refs[2 * PARTS :]
    tokens, width = att_ref.shape
    wide = width // NC // PARTS
    copies = []
    for i, src in enumerate(srcs):
        core = coords_ref[3] if i < PARTS else 1 - coords_ref[3]
        at = pl.multiple_of(core * (width // NC) + i % PARTS * wide, wide)
        for j, dst in enumerate((att_ref, dq_ref)):
            copies.append(
                pltpu.make_async_copy(
                    src.at[pl.ds(j * tokens, tokens)], dst.at[:, pl.ds(at, wide)], sems.at[2 * i + j]
                )
            )
    copy_all(copies)


def local(kernel, name, out_shape, *args, coords=None, copies=0):
    space = pl.BlockSpec(memory_space=pl.ANY if copies else pltpu.VMEM)
    smem = [] if coords is None else [pl.BlockSpec(memory_space=pltpu.SMEM)]
    return pl.pallas_call(
        kernel,
        in_specs=smem + [space] * len(args),
        out_specs=jax.tree.map(lambda _: space, out_shape),
        out_shape=out_shape,
        scratch_shapes=[pltpu.SemaphoreType.DMA((copies,))] if copies else [],
        compiler_params=pltpu.CompilerParams(vmem_limit_bytes=16 * 2**20),
        name=name,
    )(*([] if coords is None else [coords]), *args)


def fetch(coords, neighbour_ids, entry_home, cache):
    ents = cache.shape[0]
    vmem = pl.BlockSpec(memory_space=pltpu.VMEM)
    smem = pl.BlockSpec(memory_space=pltpu.SMEM)
    pieces = pl.pallas_call(
        spread_kernel,
        in_specs=[pl.BlockSpec(memory_space=pl.ANY)] * 4,
        out_specs=vmem,
        out_shape=jax.ShapeDtypeStruct((RB * FB, ents + 1, TILE_R, DH), jnp.bfloat16),
        scratch_shapes=[
            pltpu.SMEM(neighbour_ids.shape[::-1], jnp.int32),
            pltpu.SMEM(entry_home.shape, jnp.int32),
            pltpu.SemaphoreType.DMA((RB * FB + 2,)),
        ],
        compiler_params=pltpu.CompilerParams(vmem_limit_bytes=16 * 2**20),
        name="spread",
    )(
        coords,
        *(pltpu.with_memory_space_constraint(a, pltpu.HBM) for a in (neighbour_ids.T, entry_home, cache)),
    )
    store = lax.all_to_all(pieces, PLANE, split_axis=0, concat_axis=0, tiled=True)
    spots = store[:, ents, 0, :WANT].astype(jnp.int32)
    spots = spots + (spots >> 3)
    store = store.reshape(N_DB * (ents + 1), TILE_R, DH)
    picked = pl.pallas_call(
        pick_kernel,
        in_specs=[smem, vmem],
        out_specs=vmem,
        out_shape=pltpu.VMEM((N_DB * WANT, TILE_R, DH), jnp.bfloat16),
        compiler_params=pltpu.CompilerParams(vmem_limit_bytes=16 * 2**20),
        name="pick",
    )(spots, store)
    picked, coords = lax.optimization_barrier((picked, coords))
    answer = lax.all_to_all(
        picked.reshape(N_DB, WANT, TILE_R, DH), PLANE, split_axis=0, concat_axis=0, tiled=True
    )
    return answer, coords


def hops(mask, second):
    out = []
    for y in range(NY):
        for x in range(NX):
            for c in range(NC):
                to = (y, x ^ mask) if c == second else (y ^ mask, x)
                out.append(((y * NX + x) * NC + c, (to[0] * NX + to[1]) * NC + c))
    return out


def body(queries, grad_out, neighbour_ids, entry_home, cache, kv_weight):
    coords = jnp.stack([lax.axis_index(axis).astype(jnp.int32) for axis in ALL])
    tokens, width = queries.shape
    shape = jax.ShapeDtypeStruct
    swap = lambda v: lax.ppermute(v, "core", [(0, 1), (1, 0)])
    answer, coords = fetch(coords, neighbour_ids, entry_home, cache)
    hbm = lambda v: pltpu.with_memory_space_constraint(v, pltpu.HBM)
    theirs = shape((2 * tokens, width // NC), queries.dtype)
    oth = swap(local(halves_kernel, "halves", theirs, hbm(queries), hbm(grad_out), coords=coords, copies=2))
    half, quarter = FEAT // 2, FEAT // 4
    wide = width // NC // PARTS
    folded = [shape((quarter, wide), jnp.float32), shape((quarter + TILE_R, wide), jnp.int16)]
    tie = lax.optimization_barrier

    def one(keep_k, send_k, keep_v, send_v):
        return [keep_k, lax.ppermute(send_k, PLANE, hops(1, 0)), keep_v, lax.ppermute(send_v, PLANE, hops(3, 0))]

    def two(keep_k, came_k, keep_v, came_v):
        out = []
        for kept, came, mask in ((keep_k, came_k, 3), (keep_v, came_v, 1)):
            kept, sent = local(fold_kernel, "fold", folded, kept, came)
            out += [kept, lax.ppermute(sent, PLANE, hops(mask, 0))]
        return out

    args = (queries, grad_out, oth, kv_weight)
    rows = (swap(answer[:16]), swap(answer[16:]))
    laid = [pltpu.VMEM((WANT, RB, TILE_R, FEAT), jnp.bfloat16), pltpu.VMEM((FEAT, WANT * ROWS), jnp.bfloat16)]
    laid = local(own_kernel, "own_side", laid, answer, coords=coords)
    rows, laid = tie((rows, laid))
    own, other, *grads = attend(coords, rows, *laid, *args)
    sums = one(*grads)
    other = swap(other)
    sums = two(*sums)
    outs = [shape(queries.shape, queries.dtype)] * 2
    outs = local(place_kernel, "place", outs, own, other, coords=coords, copies=4)
    sums[3], outs = tie((sums[3], outs))
    part = quarter // 4
    shapes = [shape((part, width), jnp.float32)]
    shapes += [shape((part, width + 2 * PARTS * DH), jnp.int16)] * 3
    kept, *sent = local(split_kernel, "split", shapes, *sums)
    came = [lax.ppermute(v, PLANE, hops(mask, 1)) for v, mask in zip(sent, RING[1:])]
    pieces = local(join_kernel, "join", shape((NZ, 4 * part // NZ, width // 4 + DH), jnp.int16), kept, *came)
    got = lax.all_to_all(pieces, "z", split_axis=0, concat_axis=0, tiled=True)
    mine, away = local(z_kernel, "zsum", [shape((2, width), jnp.float32)] * 2, got, coords=coords)
    weight_grad = local(last_kernel, "last", shape((2, NC * width), jnp.float32), mine, swap(away), coords=coords)
    return (*outs, weight_grad)


def solution(mesh):
    grid = Mesh(mesh.devices.reshape(NZ, NY, NX, NC), ALL)
    return jax.shard_map(
        body,
        mesh=grid,
        in_specs=(P(ALL, None), P(ALL, None), P(ALL, None), P(), P(PLANE, None, None), P()),
        out_specs=(P(ALL, None), P(ALL, None), P(ALL, None)),
        check_vma=False,
    )
```
